32 devices in a mesh: parts: 2 (over y), tm: 4 (over z), chan: 4 (over x, core).
Axes of the slice: x: 2, y: 2, z: 4, core: 2. Of those that a mesh axis runs over, the one named last changes fastest.
Arguments:
- records: float32 [512, 1024], P(('parts', 'chan'), 'tm'), parts along dimension 0, may hold values from -8 to 8
- fir_taps: float32 [129], replicated, may hold values from -0.5 to 0.5
- matchings: int32 [2, 4], replicated, may hold values from 0 to 3, as said below
Outputs:
- correlograms: bfloat16 [2, 8, 64, 16448], P(None, ('parts', 'chan'), 'tm'), parts along dimension 1
The draws below stay inside these ranges and needn't reach their ends.
There are 2 independent parts, one for each index of `parts`. The reference program is written for one: setup_inputs(seed, part) draws one part's arguments, and reference() takes and returns one part's arrays. A program takes and returns all parts, laid end to end along the dimension named above; an argument that names none is the same for every part. Nothing has to cross between parts.
Inputs may be any that keep to these rules, and one draw needn't show every extreme that they name: `matchings`: each row sends every group to another group, and following a row from any group visits all 4 groups in one cycle.
All inputs are finite; a program needn't handle non-finite values.
Results may differ from the reference program's by a relative error of at most 0.0049.
Values may be sent and summed in bfloat16 or wider, within the bound.
No kernel may reach another device: no remote copies, remote signals or barrier semaphores. Data moves between devices by JAX's collectives and lax.ppermute only.
A program may use at most 64 MiB of HBM per device.

```python
import math
import jax
import jax.numpy as jnp
from jax import lax

GROUP_CH = 64
TAPS = 129
AVG = 65
MAXLAG = 128
MATCH = 2
LAGS = 257
GROUPS = 4
CHANNELS = 256
SAMPLES = 1024


def draw_matchings(key, part):
    tables_list = []
    for match_index in range(MATCH):
        visiting = jax.random.permutation(jax.random.fold_in(key, 17 + match_index), GROUPS)
        following = jnp.roll(visiting, -1)
        successor = jnp.zeros((GROUPS,), jnp.int32).at[visiting].set(following.astype(jnp.int32))
        tables_list.append(successor)
    return jnp.stack(tables_list).astype(jnp.int32)


def block_levels(key, extent, shards, low, high):
    factor_of, own = 1.0, jax.random.fold_in(key, 6)
    for dim, shards_of in shards:
        heights = jnp.exp(jax.random.uniform(jax.random.fold_in(own, dim), (shards_of,), jnp.float32, low / len(shards), high / len(shards)))
        factor_of = factor_of * jnp.repeat(heights, extent[dim] // shards_of).reshape([-1 if axis == dim else 1 for axis in range(len(extent))])
    return factor_of


def bell_draw(rng, shape, width, bound, split=(), kind=jnp.bfloat16):
    drawn = width * jax.random.normal(rng, shape, jnp.float32)
    if split:
        drawn = drawn * block_levels(rng, shape, split, -0.22, 0.18)
    return jnp.clip(drawn, -bound, bound).astype(kind)


def setup_inputs(seed: int = 0, part: int = 0) -> dict:
    keys = jax.random.split(jax.random.key(seed), 4)
    own_keys = jax.random.split(jax.random.fold_in(keys[3], part), 4)
    return {
        "records": bell_draw(own_keys[0], (CHANNELS, SAMPLES), 1.0, 8.0, ((0, 4), (1, 4)), jnp.float32),
        "fir_taps": bell_draw(keys[1], (TAPS,), TAPS ** -0.5, 0.5, (), jnp.float32),
        "matchings": draw_matchings(jax.random.fold_in(keys[3], 71), part),
    }


EPSILON = 1e-05

def preprocess(records, fir_taps):
    samples = records.shape[1]
    half_taps = fir_taps.shape[0] // 2
    padded = jnp.pad(records, ((0, 0), (half_taps, half_taps)))
    filtered = jnp.zeros_like(records)
    for tap_index in range(fir_taps.shape[0]):
        begin_at = 2 * half_taps - tap_index
        filtered = filtered + fir_taps[tap_index] * padded[:, begin_at:begin_at + samples]
    half_avg = AVG // 2
    magnitude = jnp.pad(jnp.abs(filtered), ((0, 0), (half_avg, half_avg)))
    window_sum = jnp.zeros_like(records)
    for shift_index in range(AVG):
        window_sum = window_sum + magnitude[:, shift_index:shift_index + samples]
    local_mean = window_sum / AVG
    return (filtered / (local_mean + EPSILON)).astype(jnp.bfloat16)

def correlate_group(own_rows, partner_rows):
    samples = own_rows.shape[1]
    length = samples + 2 * MAXLAG
    own_spec = jnp.fft.rfft(own_rows.astype(jnp.float32), n=length, axis=1)
    partner_spec = jnp.fft.rfft(partner_rows.astype(jnp.float32), n=length, axis=1)
    cross = jnp.conj(own_spec)[:, None, :] * partner_spec[None, :, :]
    circular = jnp.fft.irfft(cross, n=length, axis=2)
    lagged = jnp.concatenate([circular[:, :, length - MAXLAG:], circular[:, :, :MAXLAG + 1]], axis=2)
    return jnp.transpose(lagged, (0, 2, 1))

def reference(records, fir_taps, matchings):
    normed = preprocess(records, fir_taps)
    samples = records.shape[1]
    grouped = normed.reshape(GROUPS, GROUP_CH, samples)
    scaling = 1.0 / math.sqrt(samples)
    results = []
    for match_index in range(MATCH):
        partners = grouped[matchings[match_index]]
        per_group = lax.map(lambda paired: correlate_group(paired[0], paired[1]), (grouped, partners))
        shaped = (per_group * scaling).reshape(GROUPS, GROUP_CH, LAGS * GROUP_CH)
        results.append(shaped.astype(jnp.bfloat16))
    return jnp.stack(results)
```

```python
import functools
import math

import jax
import jax.numpy as jnp
from jax import lax
from jax.experimental import pallas as pl
from jax.experimental.pallas import tpu as pltpu
from jax.sharding import PartitionSpec as P

AVG = 65
MAXLAG = 128
LAGS = 257
EPSILON = 1e-05

LANES = 128
ROWS = 16
BLOCK = 256
WINDOW = BLOCK + 2 * LANES
VMEM_BYTES = 56 * 1024 * 1024


def split(values):
    high = values.astype(jnp.bfloat16)
    return high, (values - high.astype(jnp.float32)).astype(jnp.bfloat16)


def mm(left, right):
    return jnp.dot(left, right, preferred_element_type=jnp.float32)


def tap_kernel(taps_ref, high_ref, low_ref, row):
    taps = taps_ref.shape[1]
    row[...] = jnp.zeros_like(row)
    row[0:1, 0:taps] = taps_ref[...]
    spread = jnp.broadcast_to(row[0:1, :], (WINDOW, WINDOW))
    shift = (taps // 2 - LANES - taps + 1) % WINDOW
    banded = pltpu.roll(spread, shift, 1, stride=1, stride_axis=0)[:, :BLOCK]
    high, low = split(banded)
    high_ref[...] = high
    low_ref[...] = low


def filter_matrix(fir_taps):
    shape = jax.ShapeDtypeStruct((WINDOW, BLOCK), jnp.bfloat16)
    return pl.pallas_call(
        tap_kernel,
        out_shape=(shape, shape),
        scratch_shapes=[pltpu.VMEM((8, WINDOW), jnp.float32)],
        name="taps",
    )(fir_taps.reshape(1, -1))


def normalize_kernel(count, at_ref, *refs):
    blocks, (high_ref, low_ref, out_ref, padded) = refs[:count], refs[count:]
    channels, samples_dev = blocks[0].shape
    samples = samples_dev * count
    edge = jnp.zeros((channels, LANES), jnp.float32)
    padded[:, :LANES] = edge
    padded[:, LANES + samples :] = edge
    for step, block in enumerate(blocks):
        start = pl.multiple_of(LANES + at_ref[step] * samples_dev, LANES)
        padded[:, pl.ds(start, samples_dev)] = block[...]
    parts = samples // BLOCK

    def windows():
        return jnp.concatenate(
            [padded[:, n * BLOCK : n * BLOCK + WINDOW] for n in range(parts)], axis=0
        )

    high, low = split(windows())
    filtered = mm(high, high_ref[...]) + (mm(high, low_ref[...]) + mm(low, high_ref[...]))
    for n in range(parts):
        padded[:, LANES + n * BLOCK : LANES + (n + 1) * BLOCK] = jnp.abs(
            filtered[n * channels : (n + 1) * channels]
        )
    high, low = split(windows())
    rows_at = lax.broadcasted_iota(jnp.int32, (WINDOW, BLOCK), 0) - LANES
    cols_at = lax.broadcasted_iota(jnp.int32, (WINDOW, BLOCK), 1)
    band = (jnp.abs(rows_at - cols_at) <= AVG // 2).astype(jnp.float32).astype(jnp.bfloat16)
    local_mean = (mm(high, band) + mm(low, band)) * (1.0 / AVG)
    normed = (filtered / (local_mean + EPSILON)).astype(jnp.bfloat16)
    for n in range(parts):
        out_ref[:, n * BLOCK : (n + 1) * BLOCK] = normed[n * channels : (n + 1) * channels]


def normalize(blocks, places, matrix):
    channels, samples_dev = blocks[0].shape
    samples = samples_dev * len(blocks)
    return pl.pallas_call(
        functools.partial(normalize_kernel, len(blocks)),
        out_shape=jax.ShapeDtypeStruct((channels, samples), jnp.bfloat16),
        in_specs=[pl.BlockSpec(memory_space=pltpu.SMEM)]
        + [pl.BlockSpec(memory_space=pltpu.VMEM)] * (len(blocks) + 2),
        out_specs=pl.BlockSpec(memory_space=pltpu.VMEM),
        scratch_shapes=[pltpu.VMEM((channels, samples + 2 * LANES), jnp.float32)],
        compiler_params=pltpu.CompilerParams(vmem_limit_bytes=VMEM_BYTES),
        name="normalize",
    )(places, *blocks, *matrix)


def correlate_kernel(at_ref, matchings_ref, groups_ref, out_ref, partner, lagged):
    match_count = matchings_ref.shape[0]
    group_ch, samples = groups_ref.shape[1:]
    group, first = at_ref[0], pl.multiple_of(at_ref[1], ROWS)
    scaling = 1.0 / math.sqrt(samples)
    pair = 2 * group_ch
    edge = jnp.zeros((group_ch, LANES), jnp.float32)
    for match in range(match_count):
        ahead = jnp.concatenate(
            [edge, groups_ref[matchings_ref[match, group]].astype(jnp.float32)], axis=1
        )
        partner[match * pair : match * pair + group_ch, :] = ahead.astype(jnp.bfloat16)
        partner[match * pair + group_ch : (match + 1) * pair, :] = pltpu.roll(
            ahead, samples + LANES - 1, 1
        ).astype(jnp.bfloat16)
    own = jnp.concatenate(
        [
            groups_ref[group, pl.ds(first, ROWS), :].astype(jnp.float32),
            jnp.zeros((ROWS, LANES), jnp.float32),
        ],
        axis=1,
    )
    turns = LANES // 2
    per_chunk = 16
    lag_pairs = (LAGS + 1) // 2
    for chunk in range(turns // per_chunk):
        for step in range(per_chunk):
            turn = chunk * per_chunk + step
            lagged[turn * ROWS : (turn + 1) * ROWS, :] = pltpu.roll(own, 2 * turn, 1).astype(
                jnp.bfloat16
            )
        for wrap in range(-(-lag_pairs // turns)):
            left = lag_pairs - wrap * turns - chunk * per_chunk
            steps = min(per_chunk, left)
            if steps <= 0:
                continue
            depth = samples + LANES - wrap * LANES
            begin = chunk * per_chunk * ROWS
            product = lax.dot_general(
                lagged[begin : begin + steps * ROWS, :depth],
                partner[:, wrap * LANES :],
                (((1,), (1,)), ((), ())),
                preferred_element_type=jnp.float32,
            )
            product = (product * scaling).astype(jnp.bfloat16)
            for step in range(steps):
                column = (wrap * turns + chunk * per_chunk + step) * pair
                width = min(pair, LAGS * group_ch - column)
                for match in range(match_count):
                    out_ref[match, :, column : column + width] = product[
                        step * ROWS : (step + 1) * ROWS, match * pair : match * pair + width
                    ]


def correlate(groups, matchings, group, first):
    match_count = matchings.shape[0]
    _, group_ch, samples = groups.shape
    vmem = pl.BlockSpec(memory_space=pltpu.VMEM)
    smem = pl.BlockSpec(memory_space=pltpu.SMEM)
    return pl.pallas_call(
        correlate_kernel,
        out_shape=jax.ShapeDtypeStruct((match_count, ROWS, LAGS * group_ch), jnp.bfloat16),
        in_specs=[smem, smem, vmem],
        out_specs=vmem,
        scratch_shapes=[
            pltpu.VMEM((2 * match_count * group_ch, samples + LANES), jnp.bfloat16),
            pltpu.VMEM((LANES // 2 * ROWS, samples + LANES), jnp.bfloat16),
        ],
        compiler_params=pltpu.CompilerParams(vmem_limit_bytes=VMEM_BYTES),
        name="correlate",
    )(jnp.stack([group, first]), matchings, groups)


def local(records, fir_taps, matchings):
    group_ch, samples_dev = records.shape
    time_count = lax.axis_size("tm")
    time_index = lax.axis_index("tm")
    group_index = lax.axis_index("chan")
    matrix = filter_matrix(fir_taps)
    blocks = [records] + [
        lax.ppermute(records, "tm", [(i, (i + s) % time_count) for i in range(time_count)])
        for s in range(1, time_count)
    ]
    places = (time_index - jnp.arange(time_count, dtype=jnp.int32)) % time_count
    normed = normalize(blocks, places, matrix)
    groups = lax.all_gather(normed, "chan", axis=0)
    row_share = group_ch // time_count
    begin = time_index * row_share
    first = begin // ROWS * ROWS
    result = correlate(groups, matchings, group_index, first)
    if row_share != ROWS:
        result = lax.dynamic_slice_in_dim(result, begin - first, row_share, 1)
    return result[:, None]


def solution(mesh):
    in_specs = (P(("parts", "chan"), "tm"), P(), P())
    out_specs = P(None, ("parts", "chan"), "tm", None)
    return jax.shard_map(local, mesh=mesh, in_specs=in_specs, out_specs=out_specs, check_vma=False)
```

```python
import functools
import math

import jax
import jax.numpy as jnp
from jax import lax
from jax.experimental import pallas as pl
from jax.experimental.pallas import tpu as pltpu
from jax.sharding import PartitionSpec as P

AVG = 65
MAXLAG = 128
LAGS = 257
EPSILON = 1e-05

LANES = 128
ROWS = 16
BLOCK = 256
WINDOW = BLOCK + 2 * LANES
TURNS = LANES // 2
MIB = 1024 * 1024

VMEM = pl.BlockSpec(memory_space=pltpu.VMEM)
SMEM = pl.BlockSpec(memory_space=pltpu.SMEM)


def granted(*arrays):
    held = sum(math.prod(shape) * jnp.dtype(dtype).itemsize for shape, dtype in arrays)
    return pltpu.CompilerParams(vmem_limit_bytes=2 * held + 4 * MIB)


def split(values):
    high = values.astype(jnp.bfloat16)
    return high, (values - high.astype(jnp.float32)).astype(jnp.bfloat16)


def mm(left, right):
    return jnp.dot(left, right, preferred_element_type=jnp.float32)


def matrix_kernel(taps_ref, high_ref, low_ref, band_ref, row):
    taps = taps_ref.shape[1]
    row[...] = jnp.zeros_like(row)
    row[0:1, 0:taps] = taps_ref[...]
    spread = jnp.broadcast_to(row[0:1, :], (WINDOW, WINDOW))
    shift = (taps // 2 - LANES - taps + 1) % WINDOW
    banded = pltpu.roll(spread, shift, 1, stride=1, stride_axis=0)[:, :BLOCK]
    high, low = split(banded)
    high_ref[...] = high
    low_ref[...] = low
    rows_at = lax.broadcasted_iota(jnp.int32, (WINDOW, BLOCK), 0) - LANES
    cols_at = lax.broadcasted_iota(jnp.int32, (WINDOW, BLOCK), 1)
    near = jnp.abs(rows_at - cols_at) <= AVG // 2
    band_ref[...] = near.astype(jnp.float32).astype(jnp.bfloat16)


def matrices(fir_taps):
    shape = jax.ShapeDtypeStruct((WINDOW, BLOCK), jnp.bfloat16)
    return pl.pallas_call(
        matrix_kernel,
        out_shape=(shape,) * 3,
        in_specs=[VMEM],
        out_specs=(VMEM,) * 3,
        scratch_shapes=[pltpu.VMEM((8, WINDOW), jnp.float32)],
        compiler_params=granted(((WINDOW, 4 * WINDOW), jnp.float32)),
        cost_estimate=pl.CostEstimate(flops=2 * MIB, bytes_accessed=MIB, transcendentals=0),
        name="matrices",
    )(fir_taps.reshape(1, -1))


def normalize_kernel(count, *refs):
    blocks, (high_ref, low_ref, band_ref, out_ref, high, low) = refs[:count], refs[count:]
    channels, samples_dev = blocks[0].shape
    samples = samples_dev * count
    own = lax.axis_index("tm")
    edge = jnp.zeros((channels, LANES), jnp.bfloat16)
    for part in (high, low):
        part[:, :LANES] = edge
        part[:, LANES + samples :] = edge
    for step, block in enumerate(blocks):
        place = lax.rem(own + (count - step), count)
        at = pl.ds(pl.multiple_of(LANES + place * samples_dev, LANES), samples_dev)
        high[:, at], low[:, at] = split(block[...])
    parts = samples // BLOCK

    def windows(part):
        return jnp.concatenate(
            [part[:, n * BLOCK : n * BLOCK + WINDOW] for n in range(parts)], axis=0
        )

    highs, lows = windows(high), windows(low)
    filtered = mm(highs, high_ref[...]) + (mm(highs, low_ref[...]) + mm(lows, high_ref[...]))
    for n in range(parts):
        at = slice(LANES + n * BLOCK, LANES + (n + 1) * BLOCK)
        high[:, at], low[:, at] = split(jnp.abs(filtered[n * channels : (n + 1) * channels]))
    local_mean = (mm(windows(high), band_ref[...]) + mm(windows(low), band_ref[...])) * (1.0 / AVG)
    normed = (filtered / (local_mean + EPSILON)).astype(jnp.bfloat16)
    for n in range(parts):
        out_ref[:, n * BLOCK : (n + 1) * BLOCK] = normed[n * channels : (n + 1) * channels]


def normalize(blocks, banded):
    channels, samples_dev = blocks[0].shape
    samples = samples_dev * len(blocks)
    padded = (channels, samples + 2 * LANES)
    return pl.pallas_call(
        functools.partial(normalize_kernel, len(blocks)),
        out_shape=jax.ShapeDtypeStruct((channels, samples), jnp.bfloat16),
        in_specs=[VMEM] * (len(blocks) + 3),
        out_specs=VMEM,
        scratch_shapes=[pltpu.VMEM(padded, jnp.bfloat16)] * 2,
        compiler_params=granted((padded, jnp.float32), (padded, jnp.float32)),
        name="normalize",
    )(*blocks, *banded)


def lag_kernel(row_share, normed_ref, out_ref):
    first = lax.axis_index("tm") * row_share // ROWS * ROWS
    own = normed_ref[pl.ds(pl.multiple_of(first, ROWS), ROWS), :].astype(jnp.float32)
    own = jnp.concatenate([own, jnp.zeros((ROWS, LANES), jnp.float32)], axis=1)
    for turn in range(TURNS):
        out_ref[turn * ROWS : (turn + 1) * ROWS, :] = pltpu.roll(own, 2 * turn, 1).astype(
            jnp.bfloat16
        )


def lags_of(normed, row_share):
    shape = (TURNS * ROWS, normed.shape[1] + LANES)
    return pl.pallas_call(
        functools.partial(lag_kernel, row_share),
        out_shape=jax.ShapeDtypeStruct(shape, jnp.bfloat16),
        in_specs=[VMEM],
        out_specs=VMEM,
        compiler_params=granted((shape, jnp.bfloat16)),
        cost_estimate=pl.CostEstimate(flops=2 * MIB, bytes_accessed=4 * MIB, transcendentals=0),
        name="lags",
    )(normed)


def correlate_kernel(parcels, matchings_ref, lagged, *refs):
    groups, (out_ref, partner, result, sem) = refs[:parcels], refs[parcels:]
    match_count = matchings_ref.shape[0]
    group_ch, samples = groups[0].shape[-2:]
    group = lax.axis_index("chan")
    scaling = 1.0 / math.sqrt(samples)
    pair = 2 * group_ch
    edge = jnp.zeros((group_ch, LANES), jnp.float32)

    def take(match, rows):
        ahead = jnp.concatenate([edge, rows.astype(jnp.float32)], axis=1)
        partner[match * pair : match * pair + group_ch, :] = ahead.astype(jnp.bfloat16)
        partner[match * pair + group_ch : (match + 1) * pair, :] = pltpu.roll(
            ahead, samples + LANES - 1, 1
        ).astype(jnp.bfloat16)

    for match in range(match_count):
        wanted = matchings_ref[match, group]
        if parcels == 1:
            take(match, groups[0][wanted])
        else:
            for offset, held in enumerate(groups):
                pl.when((wanted ^ group) == offset)(
                    functools.partial(lambda m, h: take(m, h[...]), match, held)
                )
    lag_pairs = (LAGS + 1) // 2
    per_chunk = 16
    copies = []
    for wrap in range(-(-lag_pairs // TURNS)):
        for chunk in range(TURNS // per_chunk):
            steps = min(per_chunk, lag_pairs - wrap * TURNS - chunk * per_chunk)
            if steps <= 0:
                continue
            begin = chunk * per_chunk * ROWS
            product = lax.dot_general(
                lagged[begin : begin + steps * ROWS, : samples + LANES - wrap * LANES],
                partner[:, wrap * LANES :],
                (((1,), (1,)), ((), ())),
                preferred_element_type=jnp.float32,
            )
            product = (product * scaling).astype(jnp.bfloat16)
            left = (wrap * TURNS + chunk * per_chunk) * pair
            for step in range(steps):
                column = left + step * pair
                width = min(pair, LAGS * group_ch - column)
                for match in range(match_count):
                    result[match, :, column : column + width] = product[
                        step * ROWS : (step + 1) * ROWS, match * pair : match * pair + width
                    ]
            columns = pl.ds(left, min(steps * pair, LAGS * group_ch - left))
            copy = pltpu.make_async_copy(
                result.at[:, :, columns], out_ref.at[:, :, columns], sem.at[len(copies)]
            )
            copy.start()
            copies.append(copy)
    for copy in copies:
        copy.wait()


def correlate(matchings, lagged, groups):
    match_count = matchings.shape[0]
    group_ch, samples = groups[0].shape[-2:]
    out = (match_count, ROWS, LAGS * group_ch)
    partner = (2 * match_count * group_ch, samples + LANES)
    held = [(g.shape, g.dtype) for g in groups]
    return pl.pallas_call(
        functools.partial(correlate_kernel, len(groups)),
        out_shape=jax.ShapeDtypeStruct(out, jnp.bfloat16),
        in_specs=[SMEM, VMEM] + [VMEM] * len(groups),
        out_specs=pl.BlockSpec(memory_space=pl.ANY),
        scratch_shapes=[
            pltpu.VMEM(partner, jnp.bfloat16),
            pltpu.VMEM(out, jnp.bfloat16),
            pltpu.SemaphoreType.DMA((2 * (TURNS // ROWS) + 1,)),
        ],
        compiler_params=granted((lagged.shape, lagged.dtype), (out, jnp.bfloat16), *held),
        name="correlate",
    )(matchings, lagged, *groups)


def local(records, fir_taps, matchings):
    group_ch, samples_dev = records.shape
    time_count = lax.axis_size("tm")
    group_count = lax.axis_size("chan")
    row_share = group_ch // time_count

    def turned(cells, axis, count, step):
        return lax.ppermute(cells, axis, [(i, (i + step) % count) for i in range(count)])

    def swapped(cells, bit):
        return lax.ppermute(cells, "chan", [(i, i ^ bit) for i in range(group_count)])

    blocks = [records] + [turned(records, "tm", time_count, s) for s in range(1, time_count)]
    normed = normalize(blocks, matrices(fir_taps))
    if group_count == 4:
        far, near = swapped(normed, 2), swapped(normed, 1)
        groups = [normed, near, far, swapped(far, 1)]
    else:
        groups = [lax.all_gather(normed, "chan", axis=0)]
    result = correlate(matchings, lags_of(normed, row_share), groups)
    if row_share != ROWS:
        begin = lax.axis_index("tm") * row_share
        result = lax.dynamic_slice_in_dim(result, begin % ROWS, row_share, 1)
    return result[:, None]


def solution(mesh):
    in_specs = (P(("parts", "chan"), "tm"), P(), P())
    out_specs = P(None, ("parts", "chan"), "tm", None)
    return jax.shard_map(local, mesh=mesh, in_specs=in_specs, out_specs=out_specs, check_vma=False)
```

```python
import functools
import math

import jax
import jax.numpy as jnp
from jax import lax
from jax.experimental import pallas as pl
from jax.experimental.pallas import tpu as pltpu
from jax.sharding import PartitionSpec as P

AVG = 65
MAXLAG = 128
LAGS = 257
EPSILON = 1e-05

LANES = 128
ROWS = 16
BLOCK = 256
WINDOW = BLOCK + 2 * LANES
TURNS = LANES // 2
MIB = 1024 * 1024

VMEM = pl.BlockSpec(memory_space=pltpu.VMEM)
SMEM = pl.BlockSpec(memory_space=pltpu.SMEM)


def granted(*arrays):
    held = sum(math.prod(shape) * jnp.dtype(dtype).itemsize for shape, dtype in arrays)
    return pltpu.CompilerParams(vmem_limit_bytes=2 * held + 4 * MIB)


def split(values):
    high = values.astype(jnp.bfloat16)
    return high, (values - high.astype(jnp.float32)).astype(jnp.bfloat16)


def mm(left, right):
    return jnp.dot(left, right, preferred_element_type=jnp.float32)


def prepare_kernel(match_count, taps, packed_ref, *refs):
    high_ref, low_ref, band_ref, own_high_ref, own_low_ref, slots_ref, row = refs
    channels = own_high_ref.shape[0]
    row[...] = jnp.zeros_like(row)
    row[0:1, 0:taps] = packed_ref[channels : channels + 1, 0:taps]
    spread = jnp.broadcast_to(row[0:1, :], (WINDOW, WINDOW))
    shift = (taps // 2 - LANES - taps + 1) % WINDOW
    banded = pltpu.roll(spread, shift, 1, stride=1, stride_axis=0)[:, :BLOCK]
    high_ref[...], low_ref[...] = split(banded)
    rows_at = lax.broadcasted_iota(jnp.int32, (WINDOW, BLOCK), 0) - LANES
    cols_at = lax.broadcasted_iota(jnp.int32, (WINDOW, BLOCK), 1)
    near = jnp.abs(rows_at - cols_at) <= AVG // 2
    band_ref[...] = near.astype(jnp.float32).astype(jnp.bfloat16)
    own_high_ref[...], own_low_ref[...] = split(packed_ref[:channels, :])
    group = lax.axis_index("chan")
    here = lax.broadcasted_iota(jnp.int32, (1, LANES), 1) == group
    for match in range(match_count):
        held = packed_ref[channels + 1 + match : channels + 2 + match, :LANES]
        wanted = jnp.sum(jnp.where(here, held, 0.0), axis=1, keepdims=True).astype(jnp.int32)
        slot = (wanted ^ group).astype(jnp.float32)
        slots_ref[match] = jnp.broadcast_to(slot, slots_ref.shape[1:])


def prepare(fir_taps, records, matchings):
    channels, width = records.shape
    match_count, taps = matchings.shape[0], fir_taps.shape[0]
    rows = channels + -(-(1 + match_count) // 8) * 8

    def placed(cells, begin):
        return jnp.pad(cells, ((begin, rows - begin - cells.shape[0]), (0, width - cells.shape[1])))

    packed = (
        placed(records, 0)
        + placed(fir_taps.reshape(1, -1), channels)
        + placed(matchings.astype(jnp.float32), channels + 1)
    )
    banded = jax.ShapeDtypeStruct((WINDOW, BLOCK), jnp.bfloat16)
    own = jax.ShapeDtypeStruct(records.shape, jnp.bfloat16)
    slots = jax.ShapeDtypeStruct((match_count, channels, LANES), jnp.float32)
    outs = (banded,) * 3 + (own,) * 2 + (slots,)
    return pl.pallas_call(
        functools.partial(prepare_kernel, match_count, taps),
        out_shape=outs,
        in_specs=[VMEM],
        out_specs=(VMEM,) * len(outs),
        scratch_shapes=[pltpu.VMEM((8, WINDOW), jnp.float32)],
        compiler_params=granted(((WINDOW, 4 * WINDOW), jnp.float32)),
        cost_estimate=pl.CostEstimate(flops=2 * MIB, bytes_accessed=MIB, transcendentals=0),
        name="prepare",
    )(packed)


def normalize_kernel(steps, own_high, own_low, high_ref, low_ref, band_ref, *refs):
    blocks, (out_ref, high, low) = refs[:-3], refs[-3:]
    channels, samples_dev = own_high.shape
    count = len(blocks) + 1
    samples = samples_dev * count
    own = lax.axis_index("tm")
    edge = jnp.zeros((channels, LANES), jnp.bfloat16)
    for part in (high, low):
        part[:, :LANES] = edge
        part[:, LANES + samples :] = edge
    for step, block in zip((0, *steps), (None, *blocks)):
        place = lax.rem(own + (count - step), count)
        at = pl.ds(pl.multiple_of(LANES + place * samples_dev, LANES), samples_dev)
        if step == 0:
            high[:, at], low[:, at] = own_high[...], own_low[...]
        else:
            high[:, at], low[:, at] = split(block[...])
    parts = samples // BLOCK

    def windows(part):
        return jnp.concatenate(
            [part[:, n * BLOCK : n * BLOCK + WINDOW] for n in range(parts)], axis=0
        )

    highs, lows = windows(high), windows(low)
    filtered = mm(highs, high_ref[...]) + (mm(highs, low_ref[...]) + mm(lows, high_ref[...]))
    for n in range(parts):
        at = slice(LANES + n * BLOCK, LANES + (n + 1) * BLOCK)
        high[:, at], low[:, at] = split(jnp.abs(filtered[n * channels : (n + 1) * channels]))
    local_mean = (mm(windows(high), band_ref[...]) + mm(windows(low), band_ref[...])) * (1.0 / AVG)
    normed = (filtered / (local_mean + EPSILON)).astype(jnp.bfloat16)
    for n in range(parts):
        out_ref[:, n * BLOCK : (n + 1) * BLOCK] = normed[n * channels : (n + 1) * channels]


def normalize(own, banded, steps, blocks):
    channels, samples_dev = own[0].shape
    samples = samples_dev * (len(blocks) + 1)
    padded = (channels, samples + 2 * LANES)
    return pl.pallas_call(
        functools.partial(normalize_kernel, steps),
        out_shape=jax.ShapeDtypeStruct((channels, samples), jnp.bfloat16),
        in_specs=[VMEM] * (len(blocks) + 5),
        out_specs=VMEM,
        scratch_shapes=[pltpu.VMEM(padded, jnp.bfloat16)] * 2,
        compiler_params=granted((padded, jnp.float32), (padded, jnp.float32)),
        name="normalize",
    )(*own, *banded, *blocks)


def lag_kernel(row_share, normed_ref, out_ref):
    first = lax.axis_index("tm") * row_share // ROWS * ROWS
    own = normed_ref[pl.ds(pl.multiple_of(first, ROWS), ROWS), :].astype(jnp.float32)
    own = jnp.concatenate([own, jnp.zeros((ROWS, LANES), jnp.float32)], axis=1)
    for turn in range(TURNS):
        out_ref[turn * ROWS : (turn + 1) * ROWS, :] = pltpu.roll(own, 2 * turn, 1).astype(
            jnp.bfloat16
        )


def lags_of(normed, row_share):
    shape = (TURNS * ROWS, normed.shape[1] + LANES)
    return pl.pallas_call(
        functools.partial(lag_kernel, row_share),
        out_shape=jax.ShapeDtypeStruct(shape, jnp.bfloat16),
        in_specs=[VMEM],
        out_specs=VMEM,
        compiler_params=granted((shape, jnp.bfloat16)),
        cost_estimate=pl.CostEstimate(flops=2 * MIB, bytes_accessed=4 * MIB, transcendentals=0),
        name="lags",
    )(normed)


def correlate_kernel(parcels, picks_ref, lagged, *refs):
    groups, (out_ref, partner, result, sem) = refs[:parcels], refs[parcels:]
    match_count = picks_ref.shape[0]
    group_ch, samples = groups[0].shape[-2:]
    scaling = 1.0 / math.sqrt(samples)
    pair = 2 * group_ch
    edge = jnp.zeros((group_ch, LANES), jnp.float32)

    def take(match, rows):
        ahead = jnp.concatenate([edge, rows.astype(jnp.float32)], axis=1)
        partner[match * pair : match * pair + group_ch, :] = ahead.astype(jnp.bfloat16)
        partner[match * pair + group_ch : (match + 1) * pair, :] = pltpu.roll(
            ahead, samples + LANES - 1, 1
        ).astype(jnp.bfloat16)

    for match in range(match_count):
        if parcels == 1:
            take(match, groups[0][picks_ref[match, lax.axis_index("chan")]])
            continue
        slot = picks_ref[match]
        tiles = []
        for begin in range(0, samples, LANES):
            tile = groups[-1][:, begin : begin + LANES].astype(jnp.float32)
            for offset in range(parcels - 1):
                held = groups[offset][:, begin : begin + LANES].astype(jnp.float32)
                tile = jnp.where(slot == offset + 1.0, held, tile)
            tiles.append(tile)
        take(match, jnp.concatenate(tiles, axis=1))
    lag_pairs = (LAGS + 1) // 2
    per_chunk = 16
    copies = []
    for wrap in range(-(-lag_pairs // TURNS)):
        for chunk in range(TURNS // per_chunk):
            steps = min(per_chunk, lag_pairs - wrap * TURNS - chunk * per_chunk)
            if steps <= 0:
                continue
            begin = chunk * per_chunk * ROWS
            product = lax.dot_general(
                lagged[begin : begin + steps * ROWS, : samples + LANES - wrap * LANES],
                partner[:, wrap * LANES :],
                (((1,), (1,)), ((), ())),
                preferred_element_type=jnp.float32,
            )
            product = (product * scaling).astype(jnp.bfloat16)
            left = (wrap * TURNS + chunk * per_chunk) * pair
            for step in range(steps):
                column = left + step * pair
                width = min(pair, LAGS * group_ch - column)
                for match in range(match_count):
                    result[match, :, column : column + width] = product[
                        step * ROWS : (step + 1) * ROWS, match * pair : match * pair + width
                    ]
            columns = pl.ds(left, min(steps * pair, LAGS * group_ch - left))
            copy = pltpu.make_async_copy(
                result.at[:, :, columns], out_ref.at[:, :, columns], sem.at[len(copies)]
            )
            copy.start()
            copies.append(copy)
    for copy in copies:
        copy.wait()


def correlate(picks, lagged, groups):
    match_count = picks.shape[0]
    group_ch, samples = groups[0].shape[-2:]
    out = (match_count, ROWS, LAGS * group_ch)
    partner = (2 * match_count * group_ch, samples + LANES)
    held = [(g.shape, g.dtype) for g in groups]
    return pl.pallas_call(
        functools.partial(correlate_kernel, len(groups)),
        out_shape=jax.ShapeDtypeStruct(out, jnp.bfloat16),
        in_specs=[SMEM if len(groups) == 1 else VMEM, VMEM] + [VMEM] * len(groups),
        out_specs=pl.BlockSpec(memory_space=pl.ANY),
        scratch_shapes=[
            pltpu.VMEM(partner, jnp.bfloat16),
            pltpu.VMEM(out, jnp.bfloat16),
            pltpu.SemaphoreType.DMA((2 * (TURNS // ROWS) + 1,)),
        ],
        compiler_params=granted((lagged.shape, lagged.dtype), (out, jnp.bfloat16), *held),
        name="correlate",
    )(picks, lagged, *groups)


def local(records, fir_taps, matchings):
    group_ch, samples_dev = records.shape
    time_count = lax.axis_size("tm")
    group_count = lax.axis_size("chan")
    row_share = group_ch // time_count

    def turned(cells, axis, count, step):
        return lax.ppermute(cells, axis, [(i, (i + step) % count) for i in range(count)])

    def swapped(cells, bit):
        return lax.ppermute(cells, "chan", [(i, i ^ bit) for i in range(group_count)])

    steps = sorted(range(1, time_count), key=lambda step: (min(step, time_count - step), step % 2 * step))
    blocks = [turned(records, "tm", time_count, step) for step in steps]
    *banded, own_high, own_low, slots = prepare(fir_taps, records, matchings)
    normed = normalize((own_high, own_low), banded, steps, blocks)
    if group_count == 4:
        near, far = swapped(normed, 1), swapped(normed, 2)
        picks, groups = slots, [near, far, swapped(far, 1)]
    else:
        picks, groups = matchings, [lax.all_gather(normed, "chan", axis=0)]
    result = correlate(picks, lags_of(normed, row_share), groups)
    if row_share != ROWS:
        begin = lax.axis_index("tm") * row_share
        result = lax.dynamic_slice_in_dim(result, begin % ROWS, row_share, 1)
    return result[:, None]


def solution(mesh):
    in_specs = (P(("parts", "chan"), "tm"), P(), P())
    out_specs = P(None, ("parts", "chan"), "tm", None)
    return jax.shard_map(local, mesh=mesh, in_specs=in_specs, out_specs=out_specs, check_vma=False)
```

```python
import functools
import math

import jax
import jax.numpy as jnp
from jax import lax
from jax.experimental import pallas as pl
from jax.experimental.pallas import tpu as pltpu
from jax.sharding import PartitionSpec as P

AVG = 65
MAXLAG = 128
LAGS = 257
EPSILON = 1e-05

LANES = 128
ROWS = 16
BLOCK = 256
WINDOW = BLOCK + 2 * LANES
TURNS = LANES // 2
MIB = 1024 * 1024

VMEM = pl.BlockSpec(memory_space=pltpu.VMEM)
SMEM = pl.BlockSpec(memory_space=pltpu.SMEM)


def granted(*arrays):
    held = sum(math.prod(shape) * jnp.dtype(dtype).itemsize for shape, dtype in arrays)
    return pltpu.CompilerParams(vmem_limit_bytes=2 * held + 4 * MIB)


def split(values):
    high = values.astype(jnp.bfloat16)
    return high, (values - high.astype(jnp.float32)).astype(jnp.bfloat16)


def mm(left, right):
    return jnp.dot(left, right, preferred_element_type=jnp.float32)


def prepare_kernel(match_count, taps, packed_ref, *refs):
    high_ref, low_ref, band_ref, own_high_ref, own_low_ref, slots_ref, row = refs
    channels = own_high_ref.shape[0]
    row[...] = jnp.zeros_like(row)
    row[0:1, 0:taps] = packed_ref[channels : channels + 1, 0:taps]
    spread = jnp.broadcast_to(row[0:1, :], (WINDOW, WINDOW))
    shift = (taps // 2 - LANES - taps + 1) % WINDOW
    banded = pltpu.roll(spread, shift, 1, stride=1, stride_axis=0)[:, :BLOCK]
    high_ref[...], low_ref[...] = split(banded)
    rows_at = lax.broadcasted_iota(jnp.int32, (WINDOW, BLOCK), 0) - LANES
    cols_at = lax.broadcasted_iota(jnp.int32, (WINDOW, BLOCK), 1)
    near = jnp.abs(rows_at - cols_at) <= AVG // 2
    band_ref[...] = near.astype(jnp.float32).astype(jnp.bfloat16)
    own_high_ref[...], own_low_ref[...] = split(packed_ref[:channels, :])
    group = lax.axis_index("chan")
    here = lax.broadcasted_iota(jnp.int32, (1, LANES), 1) == group
    for match in range(match_count):
        held = packed_ref[channels + 1 + match : channels + 2 + match, :LANES]
        wanted = jnp.sum(jnp.where(here, held, 0.0), axis=1, keepdims=True).astype(jnp.int32)
        slot = (wanted ^ group).astype(jnp.float32)
        slots_ref[match] = jnp.broadcast_to(slot, slots_ref.shape[1:]).astype(jnp.bfloat16)


def prepare(fir_taps, records, matchings):
    channels, width = records.shape
    match_count, taps = matchings.shape[0], fir_taps.shape[0]
    rows = channels + -(-(1 + match_count) // 8) * 8

    def placed(cells, begin):
        return jnp.pad(cells, ((begin, rows - begin - cells.shape[0]), (0, width - cells.shape[1])))

    packed = (
        placed(records, 0)
        + placed(fir_taps.reshape(1, -1), channels)
        + placed(matchings.astype(jnp.float32), channels + 1)
    )
    banded = jax.ShapeDtypeStruct((WINDOW, BLOCK), jnp.bfloat16)
    own = jax.ShapeDtypeStruct(records.shape, jnp.bfloat16)
    slots = jax.ShapeDtypeStruct((match_count, channels, LANES), jnp.bfloat16)
    outs = (banded,) * 3 + (own,) * 2 + (slots,)
    return pl.pallas_call(
        functools.partial(prepare_kernel, match_count, taps),
        out_shape=outs,
        in_specs=[VMEM],
        out_specs=(VMEM,) * len(outs),
        scratch_shapes=[pltpu.VMEM((8, WINDOW), jnp.float32)],
        compiler_params=granted(((WINDOW, 4 * WINDOW), jnp.float32)),
        cost_estimate=pl.CostEstimate(flops=2 * MIB, bytes_accessed=MIB, transcendentals=0),
        name="prepare",
    )(packed)


def normalize_kernel(steps, own_high, own_low, high_ref, low_ref, band_ref, *refs):
    blocks, (out_ref, high, low) = refs[:-3], refs[-3:]
    channels, samples_dev = own_high.shape
    count = len(blocks) + 1
    samples = samples_dev * count
    own = lax.axis_index("tm")
    edge = jnp.zeros((channels, LANES), jnp.bfloat16)
    for part in (high, low):
        part[:, :LANES] = edge
        part[:, LANES + samples :] = edge
    for step, block in zip((0, *steps), (None, *blocks)):
        place = lax.rem(own + (count - step), count)
        at = pl.ds(pl.multiple_of(LANES + place * samples_dev, LANES), samples_dev)
        if step == 0:
            high[:, at], low[:, at] = own_high[...], own_low[...]
        else:
            high[:, at], low[:, at] = split(block[...])
    parts = samples // BLOCK

    def windows(part):
        return jnp.concatenate(
            [part[:, n * BLOCK : n * BLOCK + WINDOW] for n in range(parts)], axis=0
        )

    highs, lows = windows(high), windows(low)
    filtered = mm(highs, high_ref[...]) + (mm(highs, low_ref[...]) + mm(lows, high_ref[...]))
    for n in range(parts):
        at = slice(LANES + n * BLOCK, LANES + (n + 1) * BLOCK)
        high[:, at], low[:, at] = split(jnp.abs(filtered[n * channels : (n + 1) * channels]))
    local_mean = (mm(windows(high), band_ref[...]) + mm(windows(low), band_ref[...])) * (1.0 / AVG)
    normed = (filtered / (local_mean + EPSILON)).astype(jnp.bfloat16)
    for n in range(parts):
        out_ref[:, n * BLOCK : (n + 1) * BLOCK] = normed[n * channels : (n + 1) * channels]


def normalize(own, banded, steps, blocks):
    channels, samples_dev = own[0].shape
    samples = samples_dev * (len(blocks) + 1)
    padded = (channels, samples + 2 * LANES)
    return pl.pallas_call(
        functools.partial(normalize_kernel, steps),
        out_shape=jax.ShapeDtypeStruct((channels, samples), jnp.bfloat16),
        in_specs=[VMEM] * (len(blocks) + 5),
        out_specs=VMEM,
        scratch_shapes=[pltpu.VMEM(padded, jnp.bfloat16)] * 2,
        compiler_params=granted((padded, jnp.float32), (padded, jnp.float32)),
        name="normalize",
    )(*own, *banded, *blocks)


def lag_kernel(row_share, normed_ref, out_ref):
    first = lax.axis_index("tm") * row_share // ROWS * ROWS
    own = normed_ref[pl.ds(pl.multiple_of(first, ROWS), ROWS), :].astype(jnp.float32)
    own = jnp.concatenate([own, jnp.zeros((ROWS, LANES), jnp.float32)], axis=1)
    last = lax.broadcasted_iota(jnp.int32, (ROWS, LANES), 1) == LANES - 1
    samples = normed_ref.shape[1]
    for turn in range(TURNS):
        moved = pltpu.roll(own, 2 * turn, 1)
        tail = jnp.where(last, moved[:, :LANES], moved[:, samples:])
        at = slice(turn * ROWS, (turn + 1) * ROWS)
        out_ref[at, :samples] = moved[:, :samples].astype(jnp.bfloat16)
        out_ref[at, samples:] = tail.astype(jnp.bfloat16)


def lags_of(normed, row_share):
    shape = (TURNS * ROWS, normed.shape[1] + LANES)
    return pl.pallas_call(
        functools.partial(lag_kernel, row_share),
        out_shape=jax.ShapeDtypeStruct(shape, jnp.bfloat16),
        in_specs=[VMEM],
        out_specs=VMEM,
        compiler_params=granted((shape, jnp.bfloat16)),
        cost_estimate=pl.CostEstimate(flops=2 * MIB, bytes_accessed=4 * MIB, transcendentals=0),
        name="lags",
    )(normed)


def correlate_kernel(parcels, picks_ref, lagged, *refs):
    groups, (out_ref, partner, result, sem) = refs[:parcels], refs[parcels:]
    match_count = picks_ref.shape[0]
    group_ch, samples = groups[0].shape[-2:]
    scaling = 1.0 / math.sqrt(samples)
    pair = 2 * group_ch
    last = lax.broadcasted_iota(jnp.int32, (group_ch, LANES), 1) == LANES - 1

    def take(match, rows):
        even, odd = pl.ds(match * pair, group_ch), pl.ds(match * pair + group_ch, group_ch)
        ahead = pltpu.roll(rows.astype(jnp.float32), samples - 1, 1)
        body, end = slice(0, samples - LANES), slice(samples - LANES, samples)
        for wrap in range(2):
            partner[wrap, even, body] = rows[:, body].astype(jnp.bfloat16)
            partner[wrap, odd, body] = ahead[:, body].astype(jnp.bfloat16)
        partner[1, even, end] = rows[:, end].astype(jnp.bfloat16)
        partner[0, odd, end] = ahead[:, end].astype(jnp.bfloat16)
        partner[0, even, end] = jnp.where(last, 0.0, rows[:, end].astype(jnp.float32)).astype(jnp.bfloat16)
        partner[1, odd, end] = jnp.where(last, 0.0, ahead[:, end]).astype(jnp.bfloat16)

    for match in range(match_count):
        if parcels == 1:
            take(match, groups[0][picks_ref[match, lax.axis_index("chan")]])
            continue
        slot = picks_ref[match]
        tiles = []
        for begin in range(0, samples, LANES):
            tile = groups[-1][:, begin : begin + LANES]
            for offset in range(parcels - 1):
                held = groups[offset][:, begin : begin + LANES]
                tile = jnp.where(slot == offset + 1.0, held, tile)
            tiles.append(tile)
        take(match, jnp.concatenate(tiles, axis=1))
    lag_pairs = (LAGS + 1) // 2
    per_chunk = 16
    copies = []
    for wrap in range(-(-lag_pairs // TURNS)):
        for chunk in range(TURNS // per_chunk):
            steps = min(per_chunk, lag_pairs - wrap * TURNS - chunk * per_chunk)
            if steps <= 0:
                continue
            begin = chunk * per_chunk * ROWS
            skip = max(wrap - 1, 0) * LANES
            first = LANES if wrap == 0 else 0
            product = lax.dot_general(
                lagged[begin : begin + steps * ROWS, first : first + samples - skip],
                partner[min(wrap, 1), :, skip:],
                (((1,), (1,)), ((), ())),
                preferred_element_type=jnp.float32,
            )
            product = (product * scaling).astype(jnp.bfloat16)
            left = (wrap * TURNS + chunk * per_chunk) * pair
            for step in range(steps):
                column = left + step * pair
                width = min(pair, LAGS * group_ch - column)
                for match in range(match_count):
                    result[match, :, column : column + width] = product[
                        step * ROWS : (step + 1) * ROWS, match * pair : match * pair + width
                    ]
            columns = pl.ds(left, min(steps * pair, LAGS * group_ch - left))
            copy = pltpu.make_async_copy(
                result.at[:, :, columns], out_ref.at[:, :, columns], sem.at[len(copies)]
            )
            copy.start()
            copies.append(copy)
    for copy in copies:
        copy.wait()


def correlate(picks, lagged, groups):
    match_count = picks.shape[0]
    group_ch, samples = groups[0].shape[-2:]
    out = (match_count, ROWS, LAGS * group_ch)
    partner = (2, 2 * match_count * group_ch, samples)
    held = [(g.shape, g.dtype) for g in groups]
    return pl.pallas_call(
        functools.partial(correlate_kernel, len(groups)),
        out_shape=jax.ShapeDtypeStruct(out, jnp.bfloat16),
        in_specs=[SMEM if len(groups) == 1 else VMEM, VMEM] + [VMEM] * len(groups),
        out_specs=pl.BlockSpec(memory_space=pl.ANY),
        scratch_shapes=[
            pltpu.VMEM(partner, jnp.bfloat16),
            pltpu.VMEM(out, jnp.bfloat16),
            pltpu.SemaphoreType.DMA((2 * (TURNS // ROWS) + 1,)),
        ],
        compiler_params=granted((lagged.shape, lagged.dtype), (out, jnp.bfloat16), *held),
        name="correlate",
    )(picks, lagged, *groups)


def local(records, fir_taps, matchings):
    group_ch, samples_dev = records.shape
    time_count = lax.axis_size("tm")
    group_count = lax.axis_size("chan")
    row_share = group_ch // time_count

    def turned(cells, axis, count, step):
        return lax.ppermute(cells, axis, [(i, (i + step) % count) for i in range(count)])

    def swapped(cells, bit):
        return lax.ppermute(cells, "chan", [(i, i ^ bit) for i in range(group_count)])

    steps = sorted(range(1, time_count), key=lambda step: (min(step, time_count - step), step % 2 * step))
    blocks = [turned(records, "tm", time_count, step) for step in steps]
    *banded, own_high, own_low, slots = prepare(fir_taps, records, matchings)
    normed = normalize((own_high, own_low), banded, steps, blocks)
    if group_count == 4:
        near, far = swapped(normed, 1), swapped(normed, 2)
        picks, groups = slots, [near, far, swapped(far, 1)]
    else:
        picks, groups = matchings, [lax.all_gather(normed, "chan", axis=0)]
    result = correlate(picks, lags_of(normed, row_share), groups)
    if row_share != ROWS:
        begin = lax.axis_index("tm") * row_share
        result = lax.dynamic_slice_in_dim(result, begin % ROWS, row_share, 1)
    return result[:, None]


def solution(mesh):
    in_specs = (P(("parts", "chan"), "tm"), P(), P())
    out_specs = P(None, ("parts", "chan"), "tm", None)
    return jax.shard_map(local, mesh=mesh, in_specs=in_specs, out_specs=out_specs, check_vma=False)
```

```python
import functools
import math

import jax
import jax.numpy as jnp
from jax import lax
from jax.experimental import pallas as pl
from jax.experimental.pallas import tpu as pltpu
from jax.sharding import PartitionSpec as P

AVG = 65
MAXLAG = 128
LAGS = 257
EPSILON = 1e-05

LANES = 128
ROWS = 16
BLOCK = 256
WINDOW = BLOCK + 2 * LANES
TURNS = LANES // 2
CHUNKS = 4
MIB = 1024 * 1024

VMEM = pl.BlockSpec(memory_space=pltpu.VMEM)
SMEM = pl.BlockSpec(memory_space=pltpu.SMEM)


def granted(*arrays):
    held = sum(math.prod(shape) * jnp.dtype(dtype).itemsize for shape, dtype in arrays)
    return pltpu.CompilerParams(vmem_limit_bytes=2 * held + 4 * MIB)


def split(values):
    high = values.astype(jnp.bfloat16)
    return high, (values - high.astype(jnp.float32)).astype(jnp.bfloat16)


def mm(left, right):
    return jnp.dot(left, right, preferred_element_type=jnp.float32)


def prepare_kernel(match_count, taps, packed_ref, *refs):
    high_ref, low_ref, band_ref, own_high_ref, own_low_ref, slots_ref, row = refs
    channels = own_high_ref.shape[0]
    row[...] = jnp.zeros_like(row)
    row[0:1, 0:taps] = packed_ref[channels : channels + 1, 0:taps]
    spread = jnp.broadcast_to(row[0:1, :], (WINDOW, WINDOW))
    shift = (taps // 2 - LANES - taps + 1) % WINDOW
    banded = pltpu.roll(spread, shift, 1, stride=1, stride_axis=0)[:, :BLOCK]
    high_ref[...], low_ref[...] = split(banded)
    rows_at = lax.broadcasted_iota(jnp.int32, (WINDOW, BLOCK), 0) - LANES
    cols_at = lax.broadcasted_iota(jnp.int32, (WINDOW, BLOCK), 1)
    near = jnp.abs(rows_at - cols_at) <= AVG // 2
    band_ref[...] = near.astype(jnp.float32).astype(jnp.bfloat16)
    own_high_ref[...], own_low_ref[...] = split(packed_ref[:channels, :])
    group = lax.axis_index("chan")
    here = lax.broadcasted_iota(jnp.int32, (1, LANES), 1) == group
    for match in range(match_count):
        held = packed_ref[channels + 1 + match : channels + 2 + match, :LANES]
        wanted = jnp.sum(jnp.where(here, held, 0.0), axis=1, keepdims=True).astype(jnp.int32)
        slot = (wanted ^ group).astype(jnp.float32)
        slots_ref[match] = jnp.broadcast_to(slot, slots_ref.shape[1:]).astype(jnp.bfloat16)


def prepare(fir_taps, records, matchings):
    channels, width = records.shape
    match_count, taps = matchings.shape[0], fir_taps.shape[0]
    rows = channels + -(-(1 + match_count) // 8) * 8

    def placed(cells, begin):
        return jnp.pad(cells, ((begin, rows - begin - cells.shape[0]), (0, width - cells.shape[1])))

    packed = (
        placed(records, 0)
        + placed(fir_taps.reshape(1, -1), channels)
        + placed(matchings.astype(jnp.float32), channels + 1)
    )
    banded = jax.ShapeDtypeStruct((WINDOW, BLOCK), jnp.bfloat16)
    own = jax.ShapeDtypeStruct(records.shape, jnp.bfloat16)
    slots = jax.ShapeDtypeStruct((match_count, channels, LANES), jnp.bfloat16)
    outs = (banded,) * 3 + (own,) * 2 + (slots,)
    return pl.pallas_call(
        functools.partial(prepare_kernel, match_count, taps),
        out_shape=outs,
        in_specs=[VMEM],
        out_specs=(VMEM,) * len(outs),
        scratch_shapes=[pltpu.VMEM((8, WINDOW), jnp.float32)],
        compiler_params=granted(((WINDOW, 4 * WINDOW), jnp.float32)),
        cost_estimate=pl.CostEstimate(flops=2 * MIB, bytes_accessed=MIB, transcendentals=0),
        name="prepare",
    )(packed)


def normalize_kernel(steps, own_high, own_low, high_ref, low_ref, band_ref, *refs):
    blocks, (out_ref, high, low) = refs[:-3], refs[-3:]
    channels, samples_dev = own_high.shape
    count = len(blocks) + 1
    samples = samples_dev * count
    own = lax.axis_index("tm")
    edge = jnp.zeros((channels, LANES), jnp.bfloat16)
    for part in (high, low):
        part[:, :LANES] = edge
        part[:, LANES + samples :] = edge
    for step, block in zip((0, *steps), (None, *blocks)):
        place = lax.rem(own + (count - step), count)
        at = pl.ds(pl.multiple_of(LANES + place * samples_dev, LANES), samples_dev)
        if step == 0:
            high[:, at], low[:, at] = own_high[...], own_low[...]
        else:
            high[:, at], low[:, at] = split(block[...])
    parts = samples // BLOCK

    def windows(part):
        return jnp.concatenate(
            [part[:, n * BLOCK : n * BLOCK + WINDOW] for n in range(parts)], axis=0
        )

    highs, lows = windows(high), windows(low)
    filtered = mm(highs, high_ref[...]) + (mm(highs, low_ref[...]) + mm(lows, high_ref[...]))
    for n in range(parts):
        at = slice(LANES + n * BLOCK, LANES + (n + 1) * BLOCK)
        high[:, at], low[:, at] = split(jnp.abs(filtered[n * channels : (n + 1) * channels]))
    local_mean = (mm(windows(high), band_ref[...]) + mm(windows(low), band_ref[...])) * (1.0 / AVG)
    normed = (filtered / (local_mean + EPSILON)).astype(jnp.bfloat16)
    for n in range(parts):
        out_ref[:, n * BLOCK : (n + 1) * BLOCK] = normed[n * channels : (n + 1) * channels]


def normalize(own, banded, steps, blocks):
    channels, samples_dev = own[0].shape
    samples = samples_dev * (len(blocks) + 1)
    padded = (channels, samples + 2 * LANES)
    return pl.pallas_call(
        functools.partial(normalize_kernel, steps),
        out_shape=jax.ShapeDtypeStruct((channels, samples), jnp.bfloat16),
        in_specs=[VMEM] * (len(blocks) + 5),
        out_specs=VMEM,
        scratch_shapes=[pltpu.VMEM(padded, jnp.bfloat16)] * 2,
        compiler_params=granted((padded, jnp.float32), (padded, jnp.float32)),
        name="normalize",
    )(*own, *banded, *blocks)


def lag_kernel(row_share, normed_ref, out_ref):
    first = lax.axis_index("tm") * row_share // ROWS * ROWS
    own = normed_ref[pl.ds(pl.multiple_of(first, ROWS), ROWS), :].astype(jnp.float32)
    own = jnp.concatenate([own, jnp.zeros((ROWS, LANES), jnp.float32)], axis=1)
    last = lax.broadcasted_iota(jnp.int32, (ROWS, LANES), 1) == LANES - 1
    samples = normed_ref.shape[1]
    for turn in range(TURNS + 1):
        moved = pltpu.roll(own, 2 * turn, 1)
        tail = jnp.where(last, moved[:, :LANES], moved[:, samples:])
        at = slice(turn * ROWS, (turn + 1) * ROWS)
        out_ref[at, :samples] = moved[:, :samples].astype(jnp.bfloat16)
        out_ref[at, samples:] = tail.astype(jnp.bfloat16)


def lags_of(normed, row_share):
    shape = ((TURNS + 1) * ROWS, normed.shape[1] + LANES)
    return pl.pallas_call(
        functools.partial(lag_kernel, row_share),
        out_shape=jax.ShapeDtypeStruct(shape, jnp.bfloat16),
        in_specs=[VMEM],
        out_specs=VMEM,
        compiler_params=granted((shape, jnp.bfloat16)),
        cost_estimate=pl.CostEstimate(flops=2 * MIB, bytes_accessed=4 * MIB, transcendentals=0),
        name="lags",
    )(normed)


def correlate_kernel(parcels, picks_ref, lagged, *refs):
    groups, (out_ref, partner, result, sem) = refs[:parcels], refs[parcels:]
    match_count = picks_ref.shape[0]
    group_ch, samples = groups[0].shape[-2:]
    scaling = 1.0 / math.sqrt(samples)
    pair = 2 * group_ch
    last = lax.broadcasted_iota(jnp.int32, (group_ch, LANES), 1) == LANES - 1

    def take(match, rows):
        even, odd = pl.ds(match * pair, group_ch), pl.ds(match * pair + group_ch, group_ch)
        ahead = pltpu.roll(rows.astype(jnp.float32), samples - 1, 1)
        body, end = slice(0, samples - LANES), slice(samples - LANES, samples)
        for wrap in range(2):
            partner[wrap, even, body] = rows[:, body].astype(jnp.bfloat16)
            partner[wrap, odd, body] = ahead[:, body].astype(jnp.bfloat16)
        partner[1, even, end] = rows[:, end].astype(jnp.bfloat16)
        partner[0, odd, end] = ahead[:, end].astype(jnp.bfloat16)
        partner[0, even, end] = jnp.where(last, 0.0, rows[:, end].astype(jnp.float32)).astype(jnp.bfloat16)
        partner[1, odd, end] = jnp.where(last, 0.0, ahead[:, end]).astype(jnp.bfloat16)

    for match in range(match_count):
        if parcels == 1:
            take(match, groups[0][picks_ref[match, lax.axis_index("chan")]])
            continue
        slot = picks_ref[match]
        tiles = []
        for begin in range(0, samples, LANES):
            tile = groups[-1][:, begin : begin + LANES]
            for offset in range(parcels - 1):
                held = groups[offset][:, begin : begin + LANES]
                tile = jnp.where(slot == offset + 1.0, held, tile)
            tiles.append(tile)
        take(match, jnp.concatenate(tiles, axis=1))
    copies = []
    for wrap in range(2):
        for chunk in range(CHUNKS):
            begin = chunk * TURNS // CHUNKS
            steps = TURNS // CHUNKS + (wrap == 1 and chunk == CHUNKS - 1)
            product = lax.dot_general(
                lagged[begin * ROWS : (begin + steps) * ROWS, pl.ds((1 - wrap) * LANES, samples)],
                partner[wrap],
                (((1,), (1,)), ((), ())),
                preferred_element_type=jnp.float32,
            )
            product = (product * scaling).astype(jnp.bfloat16)
            left = (wrap * TURNS + begin) * pair
            for step in range(steps):
                column = left + step * pair
                width = min(pair, LAGS * group_ch - column)
                for match in range(match_count):
                    result[match, :, column : column + width] = product[
                        step * ROWS : (step + 1) * ROWS, match * pair : match * pair + width
                    ]
            columns = pl.ds(left, min(steps * pair, LAGS * group_ch - left))
            copy = pltpu.make_async_copy(
                result.at[:, :, columns], out_ref.at[:, :, columns], sem.at[len(copies)]
            )
            copy.start()
            copies.append(copy)
    for copy in copies:
        copy.wait()


def correlate(picks, lagged, groups):
    match_count = picks.shape[0]
    group_ch, samples = groups[0].shape[-2:]
    out = (match_count, ROWS, LAGS * group_ch)
    partner = (2, 2 * match_count * group_ch, samples)
    held = [(g.shape, g.dtype) for g in groups]
    return pl.pallas_call(
        functools.partial(correlate_kernel, len(groups)),
        out_shape=jax.ShapeDtypeStruct(out, jnp.bfloat16),
        in_specs=[SMEM if len(groups) == 1 else VMEM, VMEM] + [VMEM] * len(groups),
        out_specs=pl.BlockSpec(memory_space=pl.ANY),
        scratch_shapes=[
            pltpu.VMEM(partner, jnp.bfloat16),
            pltpu.VMEM(out, jnp.bfloat16),
            pltpu.SemaphoreType.DMA((2 * CHUNKS,)),
        ],
        compiler_params=granted((lagged.shape, lagged.dtype), (out, jnp.bfloat16), *held),
        name="correlate",
    )(picks, lagged, *groups)


def local(records, fir_taps, matchings):
    group_ch, samples_dev = records.shape
    time_count = lax.axis_size("tm")
    group_count = lax.axis_size("chan")
    row_share = group_ch // time_count

    def turned(cells, axis, count, step):
        return lax.ppermute(cells, axis, [(i, (i + step) % count) for i in range(count)])

    def swapped(cells, bit):
        return lax.ppermute(cells, "chan", [(i, i ^ bit) for i in range(group_count)])

    steps = sorted(range(1, time_count), key=lambda step: (min(step, time_count - step), step % 2 * step))
    blocks = [turned(records, "tm", time_count, step) for step in steps]
    *banded, own_high, own_low, slots = prepare(fir_taps, records, matchings)
    normed = normalize((own_high, own_low), banded, steps, blocks)
    if group_count == 4:
        near, far = swapped(normed, 1), swapped(normed, 2)
        picks, groups = slots, [near, far, swapped(far, 1)]
    else:
        picks, groups = matchings, [lax.all_gather(normed, "chan", axis=0)]
    result = correlate(picks, lags_of(normed, row_share), groups)
    if row_share != ROWS:
        begin = lax.axis_index("tm") * row_share
        result = lax.dynamic_slice_in_dim(result, begin % ROWS, row_share, 1)
    return result[:, None]


def solution(mesh):
    in_specs = (P(("parts", "chan"), "tm"), P(), P())
    out_specs = P(None, ("parts", "chan"), "tm", None)
    return jax.shard_map(local, mesh=mesh, in_specs=in_specs, out_specs=out_specs, check_vma=False)
```

```python
import functools
import math

import jax
import jax.numpy as jnp
from jax import lax
from jax.experimental import pallas as pl
from jax.experimental.pallas import tpu as pltpu
from jax.sharding import PartitionSpec as P

AVG = 65
MAXLAG = 128
LAGS = 257
EPSILON = 1e-05

LANES = 128
ROWS = 16
HALF = LANES // 2
WINDOW = 2 * LANES
TURNS = LANES // 2
CHUNKS = 4
MIB = 1024 * 1024

VMEM = pl.BlockSpec(memory_space=pltpu.VMEM)
SMEM = pl.BlockSpec(memory_space=pltpu.SMEM)


def granted(*arrays):
    held = sum(math.prod(shape) * jnp.dtype(dtype).itemsize for shape, dtype in arrays)
    return pltpu.CompilerParams(vmem_limit_bytes=2 * held + 4 * MIB)


def split(values):
    high = values.astype(jnp.bfloat16)
    return high, (values - high.astype(jnp.float32)).astype(jnp.bfloat16)


def mm(left, right):
    return jnp.dot(left, right, preferred_element_type=jnp.float32)


def prepare_kernel(match_count, taps, packed_ref, *refs):
    bands_ref, near_ref, own_high_ref, own_low_ref, slots_ref, row = refs
    channels = own_high_ref.shape[0]
    row[...] = jnp.zeros_like(row)
    row[0:1, 0:taps] = packed_ref[channels : channels + 1, 0:taps]
    spread = jnp.broadcast_to(row[0:1, :], (WINDOW, 2 * WINDOW))
    shift = 2 * WINDOW - HALF - taps // 2
    banded = pltpu.roll(spread, shift, 1, stride=1, stride_axis=0)[:, :LANES]
    bands_ref[:, :LANES], bands_ref[:, LANES:] = split(banded)
    rows_at = lax.broadcasted_iota(jnp.int32, (WINDOW, LANES), 0) - HALF
    cols_at = lax.broadcasted_iota(jnp.int32, (WINDOW, LANES), 1)
    near = jnp.abs(rows_at - cols_at) <= AVG // 2
    near_ref[...] = near.astype(jnp.float32).astype(jnp.bfloat16)
    own_high_ref[...], own_low_ref[...] = split(packed_ref[:channels, :])
    group = lax.axis_index("chan")
    here = lax.broadcasted_iota(jnp.int32, (1, LANES), 1) == group
    for match in range(match_count):
        held = packed_ref[channels + 1 + match : channels + 2 + match, :LANES]
        wanted = jnp.sum(jnp.where(here, held, 0.0), axis=1, keepdims=True).astype(jnp.int32)
        slot = (wanted ^ group).astype(jnp.float32)
        slots_ref[match] = jnp.broadcast_to(slot, slots_ref.shape[1:]).astype(jnp.bfloat16)


def prepare(fir_taps, records, matchings):
    channels, width = records.shape
    match_count, taps = matchings.shape[0], fir_taps.shape[0]
    rows = channels + -(-(1 + match_count) // 8) * 8

    def placed(cells, begin):
        return jnp.pad(cells, ((begin, rows - begin - cells.shape[0]), (0, width - cells.shape[1])))

    packed = (
        placed(records, 0)
        + placed(fir_taps.reshape(1, -1), channels)
        + placed(matchings.astype(jnp.float32), channels + 1)
    )
    bands = jax.ShapeDtypeStruct((WINDOW, 2 * LANES), jnp.bfloat16)
    near = jax.ShapeDtypeStruct((WINDOW, LANES), jnp.bfloat16)
    own = jax.ShapeDtypeStruct(records.shape, jnp.bfloat16)
    slots = jax.ShapeDtypeStruct((match_count, channels, LANES), jnp.bfloat16)
    outs = (bands, near, own, own, slots)
    return pl.pallas_call(
        functools.partial(prepare_kernel, match_count, taps),
        out_shape=outs,
        in_specs=[VMEM],
        out_specs=(VMEM,) * len(outs),
        scratch_shapes=[pltpu.VMEM((8, 2 * WINDOW), jnp.float32)],
        compiler_params=granted(((WINDOW, 4 * WINDOW), jnp.float32)),
        cost_estimate=pl.CostEstimate(flops=2 * MIB, bytes_accessed=MIB, transcendentals=0),
        name="prepare",
    )(packed)


def normalize_kernel(steps, own_high, own_low, bands_ref, near_ref, *refs):
    blocks, (out_ref, high, low) = refs[:-3], refs[-3:]
    channels, samples_dev = own_high.shape
    count = len(blocks) + 1
    samples = samples_dev * count
    own = lax.axis_index("tm")
    edge = jnp.zeros((channels, LANES), jnp.bfloat16)
    for part in (high, low):
        part[:, :LANES] = edge
        part[:, LANES + samples :] = edge
    for step, block in zip((0, *steps), (None, *blocks)):
        place = lax.rem(own + (count - step), count)
        at = pl.ds(pl.multiple_of(LANES + place * samples_dev, LANES), samples_dev)
        if step == 0:
            high[:, at], low[:, at] = own_high[...], own_low[...]
        else:
            high[:, at], low[:, at] = split(block[...])
    tiles = samples // LANES

    def windows(part, count):
        return jnp.concatenate(
            [part[:, n * LANES : n * LANES + WINDOW] for n in range(count)], axis=0
        )

    product = mm(windows(high, tiles + 1), bands_ref[...])
    product = product[:, :LANES] + (
        product[:, LANES:] + mm(windows(low, tiles + 1), bands_ref[:, :LANES])
    )
    early = lax.broadcasted_iota(jnp.int32, (channels, LANES), 1) < HALF
    turned = []
    for n in range(tiles + 1):
        filtered = product[n * channels : (n + 1) * channels]
        if n == 0:
            filtered = jnp.where(early, 0.0, filtered)
        if n == tiles:
            filtered = jnp.where(early, filtered, 0.0)
        at = slice(n * LANES, (n + 1) * LANES)
        high[:, at], low[:, at] = split(jnp.abs(filtered))
        turned.append(pltpu.roll(filtered, HALF, 1))
    sums = mm(windows(high, tiles), near_ref[...]) + mm(windows(low, tiles), near_ref[...])
    for n in range(tiles):
        filtered = jnp.where(early, turned[n], turned[n + 1])
        local_mean = sums[n * channels : (n + 1) * channels] * (1.0 / AVG)
        out_ref[:, n * LANES : (n + 1) * LANES] = (filtered / (local_mean + EPSILON)).astype(
            jnp.bfloat16
        )


def normalize(own, banded, steps, blocks):
    channels, samples_dev = own[0].shape
    samples = samples_dev * (len(blocks) + 1)
    padded = (channels, samples + 2 * LANES)
    return pl.pallas_call(
        functools.partial(normalize_kernel, steps),
        out_shape=jax.ShapeDtypeStruct((channels, samples), jnp.bfloat16),
        in_specs=[VMEM] * (len(blocks) + 4),
        out_specs=VMEM,
        scratch_shapes=[pltpu.VMEM(padded, jnp.bfloat16)] * 2,
        compiler_params=granted((padded, jnp.float32), (padded, jnp.float32)),
        name="normalize",
    )(*own, *banded, *blocks)


def lag_kernel(row_share, normed_ref, out_ref):
    first = lax.axis_index("tm") * row_share // ROWS * ROWS
    own = normed_ref[pl.ds(pl.multiple_of(first, ROWS), ROWS), :].astype(jnp.float32)
    own = jnp.concatenate([own, jnp.zeros((ROWS, LANES), jnp.float32)], axis=1)
    last = lax.broadcasted_iota(jnp.int32, (ROWS, LANES), 1) == LANES - 1
    samples = normed_ref.shape[1]
    for turn in range(TURNS + 1):
        moved = pltpu.roll(own, 2 * turn, 1)
        tail = jnp.where(last, moved[:, :LANES], moved[:, samples:])
        at = slice(turn * ROWS, (turn + 1) * ROWS)
        out_ref[at, :samples] = moved[:, :samples].astype(jnp.bfloat16)
        out_ref[at, samples:] = tail.astype(jnp.bfloat16)


def lags_of(normed, row_share):
    shape = ((TURNS + 1) * ROWS, normed.shape[1] + LANES)
    return pl.pallas_call(
        functools.partial(lag_kernel, row_share),
        out_shape=jax.ShapeDtypeStruct(shape, jnp.bfloat16),
        in_specs=[VMEM],
        out_specs=VMEM,
        compiler_params=granted((shape, jnp.bfloat16)),
        cost_estimate=pl.CostEstimate(flops=2 * MIB, bytes_accessed=4 * MIB, transcendentals=0),
        name="lags",
    )(normed)


def correlate_kernel(parcels, picks_ref, lagged, *refs):
    groups, (out_ref, partner, result, sem) = refs[:parcels], refs[parcels:]
    match_count = picks_ref.shape[0]
    group_ch, samples = groups[0].shape[-2:]
    scaling = 1.0 / math.sqrt(samples)
    pair = 2 * group_ch
    last = lax.broadcasted_iota(jnp.int32, (group_ch, LANES), 1) == LANES - 1

    def take(match, rows):
        even, odd = pl.ds(match * pair, group_ch), pl.ds(match * pair + group_ch, group_ch)
        ahead = pltpu.roll(rows.astype(jnp.float32), samples - 1, 1)
        body, end = slice(0, samples - LANES), slice(samples - LANES, samples)
        for wrap in range(2):
            partner[wrap, even, body] = rows[:, body].astype(jnp.bfloat16)
            partner[wrap, odd, body] = ahead[:, body].astype(jnp.bfloat16)
        partner[1, even, end] = rows[:, end].astype(jnp.bfloat16)
        partner[0, odd, end] = ahead[:, end].astype(jnp.bfloat16)
        partner[0, even, end] = jnp.where(last, 0.0, rows[:, end].astype(jnp.float32)).astype(jnp.bfloat16)
        partner[1, odd, end] = jnp.where(last, 0.0, ahead[:, end]).astype(jnp.bfloat16)

    for match in range(match_count):
        if parcels == 1:
            take(match, groups[0][picks_ref[match, lax.axis_index("chan")]])
            continue
        slot = picks_ref[match]
        tiles = []
        for begin in range(0, samples, LANES):
            tile = groups[-1][:, begin : begin + LANES]
            for offset in range(parcels - 1):
                held = groups[offset][:, begin : begin + LANES]
                tile = jnp.where(slot == offset + 1.0, held, tile)
            tiles.append(tile)
        take(match, jnp.concatenate(tiles, axis=1))
    copies = []
    for wrap in (1, 0):
        for chunk in range(CHUNKS):
            begin = chunk * TURNS // CHUNKS
            steps = TURNS // CHUNKS + (wrap == 1 and chunk == CHUNKS - 1)
            product = lax.dot_general(
                lagged[begin * ROWS : (begin + steps) * ROWS, pl.ds((1 - wrap) * LANES, samples)],
                partner[wrap],
                (((1,), (1,)), ((), ())),
                preferred_element_type=jnp.float32,
            )
            product = (product * scaling).astype(jnp.bfloat16)
            left = (wrap * TURNS + begin) * pair
            for step in range(steps):
                column = left + step * pair
                width = min(pair, LAGS * group_ch - column)
                for match in range(match_count):
                    result[match, :, column : column + width] = product[
                        step * ROWS : (step + 1) * ROWS, match * pair : match * pair + width
                    ]
            columns = pl.ds(left, min(steps * pair, LAGS * group_ch - left))
            copy = pltpu.make_async_copy(
                result.at[:, :, columns], out_ref.at[:, :, columns], sem.at[len(copies)]
            )
            copy.start()
            copies.append(copy)
    for copy in copies:
        copy.wait()


def correlate(picks, lagged, groups):
    match_count = picks.shape[0]
    group_ch, samples = groups[0].shape[-2:]
    out = (match_count, ROWS, LAGS * group_ch)
    partner = (2, 2 * match_count * group_ch, samples)
    held = [(g.shape, g.dtype) for g in groups]
    return pl.pallas_call(
        functools.partial(correlate_kernel, len(groups)),
        out_shape=jax.ShapeDtypeStruct(out, jnp.bfloat16),
        in_specs=[SMEM if len(groups) == 1 else VMEM, VMEM] + [VMEM] * len(groups),
        out_specs=pl.BlockSpec(memory_space=pl.ANY),
        scratch_shapes=[
            pltpu.VMEM(partner, jnp.bfloat16),
            pltpu.VMEM(out, jnp.bfloat16),
            pltpu.SemaphoreType.DMA((2 * CHUNKS,)),
        ],
        compiler_params=granted((lagged.shape, lagged.dtype), (out, jnp.bfloat16), *held),
        name="correlate",
    )(picks, lagged, *groups)


def local(records, fir_taps, matchings):
    group_ch, samples_dev = records.shape
    time_count = lax.axis_size("tm")
    group_count = lax.axis_size("chan")
    row_share = group_ch // time_count

    def turned(cells, axis, count, step):
        return lax.ppermute(cells, axis, [(i, (i + step) % count) for i in range(count)])

    def swapped(cells, bit):
        return lax.ppermute(cells, "chan", [(i, i ^ bit) for i in range(group_count)])

    steps = sorted(range(1, time_count), key=lambda step: (min(step, time_count - step), step % 2 * step))
    blocks = [turned(records, "tm", time_count, step) for step in steps]
    *banded, own_high, own_low, slots = prepare(fir_taps, records, matchings)
    normed = normalize((own_high, own_low), banded, steps, blocks)
    if group_count == 4:
        near, far = swapped(normed, 1), swapped(normed, 2)
        picks, groups = slots, [near, far, swapped(far, 1)]
    else:
        picks, groups = matchings, [lax.all_gather(normed, "chan", axis=0)]
    result = correlate(picks, lags_of(normed, row_share), groups)
    if row_share != ROWS:
        begin = lax.axis_index("tm") * row_share
        result = lax.dynamic_slice_in_dim(result, begin % ROWS, row_share, 1)
    return result[:, None]


def solution(mesh):
    in_specs = (P(("parts", "chan"), "tm"), P(), P())
    out_specs = P(None, ("parts", "chan"), "tm", None)
    return jax.shard_map(local, mesh=mesh, in_specs=in_specs, out_specs=out_specs, check_vma=False)
```

```python
import functools
import math

import jax
import jax.numpy as jnp
from jax import lax
from jax.experimental import pallas as pl
from jax.experimental.pallas import tpu as pltpu
from jax.sharding import PartitionSpec as P

AVG = 65
MAXLAG = 128
LAGS = 257
EPSILON = 1e-05

LANES = 128
ROWS = 16
HALF = LANES // 2
WINDOW = 2 * LANES
TURNS = LANES // 2
CHUNKS = 4
MIB = 1024 * 1024

VMEM = pl.BlockSpec(memory_space=pltpu.VMEM)
SMEM = pl.BlockSpec(memory_space=pltpu.SMEM)


def granted(*arrays):
    held = sum(math.prod(shape) * jnp.dtype(dtype).itemsize for shape, dtype in arrays)
    return pltpu.CompilerParams(vmem_limit_bytes=2 * held + 4 * MIB)


def split(values):
    high = values.astype(jnp.bfloat16)
    return high, (values - high.astype(jnp.float32)).astype(jnp.bfloat16)


def mm(left, right):
    return jnp.dot(left, right, preferred_element_type=jnp.float32)


def prepare_kernel(match_count, taps, packed_ref, *refs):
    bands_ref, near_ref, own_high_ref, own_low_ref, slots_ref, row = refs
    channels = own_high_ref.shape[0]
    row[...] = jnp.zeros_like(row)
    row[0:1, 0:taps] = packed_ref[channels : channels + 1, 0:taps]
    spread = jnp.broadcast_to(row[0:1, :], (WINDOW, 2 * WINDOW))
    shift = 2 * WINDOW - HALF - taps // 2
    banded = pltpu.roll(spread, shift, 1, stride=1, stride_axis=0)[:, :LANES]
    bands_ref[:, :LANES], bands_ref[:, LANES:] = split(banded)
    rows_at = lax.broadcasted_iota(jnp.int32, (WINDOW, LANES), 0) - HALF
    cols_at = lax.broadcasted_iota(jnp.int32, (WINDOW, LANES), 1)
    near = jnp.abs(rows_at - cols_at) <= AVG // 2
    near_ref[...] = near.astype(jnp.float32).astype(jnp.bfloat16)
    own_high_ref[...], own_low_ref[...] = split(packed_ref[:channels, :])
    group = lax.axis_index("chan")
    here = lax.broadcasted_iota(jnp.int32, (1, LANES), 1) == group
    for match in range(match_count):
        held = packed_ref[channels + 1 + match : channels + 2 + match, :LANES]
        wanted = jnp.sum(jnp.where(here, held, 0.0), axis=1, keepdims=True).astype(jnp.int32)
        slot = (wanted ^ group).astype(jnp.float32)
        slots_ref[match] = jnp.broadcast_to(slot, slots_ref.shape[1:]).astype(jnp.bfloat16)


def prepare(fir_taps, records, matchings):
    channels, width = records.shape
    match_count, taps = matchings.shape[0], fir_taps.shape[0]
    rows = channels + -(-(1 + match_count) // 8) * 8

    def placed(cells, begin):
        return jnp.pad(cells, ((begin, rows - begin - cells.shape[0]), (0, width - cells.shape[1])))

    packed = (
        placed(records, 0)
        + placed(fir_taps.reshape(1, -1), channels)
        + placed(matchings.astype(jnp.float32), channels + 1)
    )
    bands = jax.ShapeDtypeStruct((WINDOW, 2 * LANES), jnp.bfloat16)
    near = jax.ShapeDtypeStruct((WINDOW, LANES), jnp.bfloat16)
    own = jax.ShapeDtypeStruct(records.shape, jnp.bfloat16)
    slots = jax.ShapeDtypeStruct((match_count, channels, LANES), jnp.bfloat16)
    outs = (bands, near, own, own, slots)
    return pl.pallas_call(
        functools.partial(prepare_kernel, match_count, taps),
        out_shape=outs,
        in_specs=[VMEM],
        out_specs=(VMEM,) * len(outs),
        scratch_shapes=[pltpu.VMEM((8, 2 * WINDOW), jnp.float32)],
        compiler_params=granted(((WINDOW, 4 * WINDOW), jnp.float32)),
        cost_estimate=pl.CostEstimate(flops=2 * MIB, bytes_accessed=MIB, transcendentals=0),
        name="prepare",
    )(packed)


def normalize_kernel(steps, own_high, own_low, bands_ref, near_ref, *refs):
    blocks, (out_ref, high, low) = refs[:-3], refs[-3:]
    channels, samples_dev = own_high.shape
    count = len(blocks) + 1
    samples = samples_dev * count
    own = lax.axis_index("tm")
    edge = jnp.zeros((channels, LANES), jnp.bfloat16)
    for part in (high, low):
        part[:, :LANES] = edge
        part[:, LANES + samples :] = edge
    for step, block in zip((0, *steps), (None, *blocks)):
        place = lax.rem(own + (count - step), count)
        at = pl.ds(pl.multiple_of(LANES + place * samples_dev, LANES), samples_dev)
        if step == 0:
            high[:, at], low[:, at] = own_high[...], own_low[...]
        else:
            high[:, at], low[:, at] = split(block[...])
    tiles = samples // LANES

    def windows(part, count):
        return jnp.concatenate(
            [part[:, n * LANES : n * LANES + WINDOW] for n in range(count)], axis=0
        )

    product = mm(windows(high, tiles + 1), bands_ref[...])
    product = product[:, :LANES] + (
        product[:, LANES:] + mm(windows(low, tiles + 1), bands_ref[:, :LANES])
    )
    early = lax.broadcasted_iota(jnp.int32, (channels, LANES), 1) < HALF
    turned = []
    for n in range(tiles + 1):
        filtered = product[n * channels : (n + 1) * channels]
        if n == 0:
            filtered = jnp.where(early, 0.0, filtered)
        if n == tiles:
            filtered = jnp.where(early, filtered, 0.0)
        at = slice(n * LANES, (n + 1) * LANES)
        high[:, at], low[:, at] = split(jnp.abs(filtered))
        turned.append(pltpu.roll(filtered, HALF, 1))
    sums = mm(windows(high, tiles), near_ref[...]) + mm(windows(low, tiles), near_ref[...])
    for n in range(tiles):
        filtered = jnp.where(early, turned[n], turned[n + 1])
        local_mean = sums[n * channels : (n + 1) * channels] * (1.0 / AVG)
        out_ref[:, n * LANES : (n + 1) * LANES] = (filtered / (local_mean + EPSILON)).astype(
            jnp.bfloat16
        )


def normalize(own, banded, steps, blocks):
    channels, samples_dev = own[0].shape
    samples = samples_dev * (len(blocks) + 1)
    padded = (channels, samples + 2 * LANES)
    return pl.pallas_call(
        functools.partial(normalize_kernel, steps),
        out_shape=jax.ShapeDtypeStruct((channels, samples), jnp.bfloat16),
        in_specs=[VMEM] * (len(blocks) + 4),
        out_specs=VMEM,
        scratch_shapes=[pltpu.VMEM(padded, jnp.bfloat16)] * 2,
        compiler_params=granted((padded, jnp.float32), (padded, jnp.float32)),
        name="normalize",
    )(*own, *banded, *blocks)


def lag_kernel(row_share, normed_ref, out_ref):
    first = lax.axis_index("tm") * row_share // ROWS * ROWS
    own = normed_ref[pl.ds(pl.multiple_of(first, ROWS), ROWS), :].astype(jnp.float32)
    own = jnp.concatenate([own, jnp.zeros((ROWS, LANES), jnp.float32)], axis=1)
    last = lax.broadcasted_iota(jnp.int32, (ROWS, LANES), 1) == LANES - 1
    samples = normed_ref.shape[1]
    for turn in range(TURNS + 1):
        moved = pltpu.roll(own, 2 * turn, 1)
        tail = jnp.where(last, moved[:, :LANES], moved[:, samples:])
        at = slice(turn * ROWS, (turn + 1) * ROWS)
        out_ref[at, :samples] = moved[:, :samples].astype(jnp.bfloat16)
        out_ref[at, samples:] = tail.astype(jnp.bfloat16)


def lags_of(normed, row_share):
    shape = ((TURNS + 1) * ROWS, normed.shape[1] + LANES)
    return pl.pallas_call(
        functools.partial(lag_kernel, row_share),
        out_shape=jax.ShapeDtypeStruct(shape, jnp.bfloat16),
        in_specs=[VMEM],
        out_specs=VMEM,
        compiler_params=granted((shape, jnp.bfloat16)),
        cost_estimate=pl.CostEstimate(flops=2 * MIB, bytes_accessed=4 * MIB, transcendentals=0),
        name="lags",
    )(normed)


def correlate_kernel(parcels, picks_ref, lagged, *refs):
    groups, (out_ref, partner, first_end, result, sem) = refs[:parcels], refs[parcels:]
    match_count = picks_ref.shape[0]
    group_ch, samples = groups[0].shape[-2:]
    scaling = 1.0 / math.sqrt(samples)
    pair = 2 * group_ch
    last = lax.broadcasted_iota(jnp.int32, (group_ch, LANES), 1) == LANES - 1

    def take(match, rows):
        even, odd = pl.ds(match * pair, group_ch), pl.ds(match * pair + group_ch, group_ch)
        ahead = pltpu.roll(rows.astype(jnp.float32), samples - 1, 1)
        end = slice(samples - LANES, samples)
        partner[even, :] = rows.astype(jnp.bfloat16)
        partner[odd, : samples - LANES] = ahead[:, : samples - LANES].astype(jnp.bfloat16)
        partner[odd, end] = jnp.where(last, 0.0, ahead[:, end]).astype(jnp.bfloat16)
        first_end[even, :] = jnp.where(last, 0.0, rows[:, end].astype(jnp.float32)).astype(jnp.bfloat16)
        first_end[odd, :] = ahead[:, end].astype(jnp.bfloat16)

    for match in range(match_count):
        if parcels == 1:
            take(match, groups[0][picks_ref[match, lax.axis_index("chan")]])
            continue
        slot = picks_ref[match]
        tiles = []
        for begin in range(0, samples, LANES):
            tile = groups[-1][:, begin : begin + LANES]
            for offset in range(parcels - 1):
                held = groups[offset][:, begin : begin + LANES]
                tile = jnp.where(slot == offset + 1.0, held, tile)
            tiles.append(tile)
        take(match, jnp.concatenate(tiles, axis=1))
    copies = []
    for wrap in (1, 0):
        if wrap == 0:
            partner[:, samples - LANES :] = first_end[...]
        for chunk in range(CHUNKS):
            begin = chunk * TURNS // CHUNKS
            steps = TURNS // CHUNKS + (wrap == 1 and chunk == CHUNKS - 1)
            product = lax.dot_general(
                lagged[begin * ROWS : (begin + steps) * ROWS, pl.ds((1 - wrap) * LANES, samples)],
                partner[...],
                (((1,), (1,)), ((), ())),
                preferred_element_type=jnp.float32,
            )
            product = (product * scaling).astype(jnp.bfloat16)
            left = (wrap * TURNS + begin) * pair
            for step in range(steps):
                column = left + step * pair
                width = min(pair, LAGS * group_ch - column)
                for match in range(match_count):
                    result[match, :, column : column + width] = product[
                        step * ROWS : (step + 1) * ROWS, match * pair : match * pair + width
                    ]
            columns = pl.ds(left, min(steps * pair, LAGS * group_ch - left))
            copy = pltpu.make_async_copy(
                result.at[:, :, columns], out_ref.at[:, :, columns], sem.at[len(copies)]
            )
            copy.start()
            copies.append(copy)
    for copy in copies:
        copy.wait()


def correlate(picks, lagged, groups):
    match_count = picks.shape[0]
    group_ch, samples = groups[0].shape[-2:]
    out = (match_count, ROWS, LAGS * group_ch)
    partner = (2 * match_count * group_ch, samples)
    held = [(g.shape, g.dtype) for g in groups]
    return pl.pallas_call(
        functools.partial(correlate_kernel, len(groups)),
        out_shape=jax.ShapeDtypeStruct(out, jnp.bfloat16),
        in_specs=[SMEM if len(groups) == 1 else VMEM, VMEM] + [VMEM] * len(groups),
        out_specs=pl.BlockSpec(memory_space=pl.ANY),
        scratch_shapes=[
            pltpu.VMEM(partner, jnp.bfloat16),
            pltpu.VMEM((partner[0], LANES), jnp.bfloat16),
            pltpu.VMEM(out, jnp.bfloat16),
            pltpu.SemaphoreType.DMA((2 * CHUNKS,)),
        ],
        compiler_params=granted((lagged.shape, lagged.dtype), (out, jnp.bfloat16), *held),
        name="correlate",
    )(picks, lagged, *groups)


def local(records, fir_taps, matchings):
    group_ch, samples_dev = records.shape
    time_count = lax.axis_size("tm")
    group_count = lax.axis_size("chan")
    row_share = group_ch // time_count

    def turned(cells, axis, count, step):
        return lax.ppermute(cells, axis, [(i, (i + step) % count) for i in range(count)])

    def swapped(cells, bit):
        return lax.ppermute(cells, "chan", [(i, i ^ bit) for i in range(group_count)])

    steps = sorted(range(1, time_count), key=lambda step: (min(step, time_count - step), step % 2 * step))
    blocks = [turned(records, "tm", time_count, step) for step in steps]
    *banded, own_high, own_low, slots = prepare(fir_taps, records, matchings)
    normed = normalize((own_high, own_low), banded, steps, blocks)
    if group_count == 4:
        near, far = swapped(normed, 1), swapped(normed, 2)
        picks, groups = slots, [near, far, swapped(far, 1)]
    else:
        picks, groups = matchings, [lax.all_gather(normed, "chan", axis=0)]
    result = correlate(picks, lags_of(normed, row_share), groups)
    if row_share != ROWS:
        begin = lax.axis_index("tm") * row_share
        result = lax.dynamic_slice_in_dim(result, begin % ROWS, row_share, 1)
    return result[:, None]


def solution(mesh):
    in_specs = (P(("parts", "chan"), "tm"), P(), P())
    out_specs = P(None, ("parts", "chan"), "tm", None)
    return jax.shard_map(local, mesh=mesh, in_specs=in_specs, out_specs=out_specs, check_vma=False)
```

```python
import functools
import math

import jax
import jax.numpy as jnp
from jax import lax
from jax.experimental import pallas as pl
from jax.experimental.pallas import tpu as pltpu
from jax.sharding import PartitionSpec as P

AVG = 65
MAXLAG = 128
LAGS = 257
EPSILON = 1e-05

LANES = 128
ROWS = 16
HALF = LANES // 2
WINDOW = 2 * LANES
TURNS = LANES // 2
CHUNKS = 4
MIB = 1024 * 1024

VMEM = pl.BlockSpec(memory_space=pltpu.VMEM)
SMEM = pl.BlockSpec(memory_space=pltpu.SMEM)


def granted(*arrays):
    held = sum(math.prod(shape) * jnp.dtype(dtype).itemsize for shape, dtype in arrays)
    return pltpu.CompilerParams(vmem_limit_bytes=2 * held + 4 * MIB)


def split(values):
    high = values.astype(jnp.bfloat16)
    return high, (values - high.astype(jnp.float32)).astype(jnp.bfloat16)


def mm(left, right):
    return jnp.dot(left, right, preferred_element_type=jnp.float32)


def prepare_kernel(match_count, taps, packed_ref, *refs):
    bands_ref, near_ref, own_high_ref, own_low_ref, slots_ref, row = refs
    channels = own_high_ref.shape[0]
    row[...] = jnp.zeros_like(row)
    row[0:1, 0:taps] = packed_ref[channels : channels + 1, 0:taps]
    spread = jnp.broadcast_to(row[0:1, :], (WINDOW, 2 * WINDOW))
    shift = 2 * WINDOW - HALF - taps // 2
    banded = pltpu.roll(spread, shift, 1, stride=1, stride_axis=0)[:, :LANES]
    bands_ref[:, :LANES], bands_ref[:, LANES:] = split(banded)
    rows_at = lax.broadcasted_iota(jnp.int32, (WINDOW, LANES), 0) - HALF
    cols_at = lax.broadcasted_iota(jnp.int32, (WINDOW, LANES), 1)
    near = jnp.abs(rows_at - cols_at) <= AVG // 2
    near_ref[...] = near.astype(jnp.float32).astype(jnp.bfloat16)
    own_high_ref[...], own_low_ref[...] = split(packed_ref[:channels, :])
    group = lax.axis_index("chan")
    here = lax.broadcasted_iota(jnp.int32, (1, LANES), 1) == group
    for match in range(match_count):
        held = packed_ref[channels + 1 + match : channels + 2 + match, :LANES]
        wanted = jnp.sum(jnp.where(here, held, 0.0), axis=1, keepdims=True).astype(jnp.int32)
        slot = (wanted ^ group).astype(jnp.float32)
        slots_ref[match] = jnp.broadcast_to(slot, slots_ref.shape[1:]).astype(jnp.bfloat16)


def prepare(fir_taps, records, matchings):
    channels, width = records.shape
    match_count, taps = matchings.shape[0], fir_taps.shape[0]
    rows = channels + -(-(1 + match_count) // 8) * 8

    def placed(cells, begin):
        return jnp.pad(cells, ((begin, rows - begin - cells.shape[0]), (0, width - cells.shape[1])))

    packed = (
        placed(records, 0)
        + placed(fir_taps.reshape(1, -1), channels)
        + placed(matchings.astype(jnp.float32), channels + 1)
    )
    bands = jax.ShapeDtypeStruct((WINDOW, 2 * LANES), jnp.bfloat16)
    near = jax.ShapeDtypeStruct((WINDOW, LANES), jnp.bfloat16)
    own = jax.ShapeDtypeStruct(records.shape, jnp.bfloat16)
    slots = jax.ShapeDtypeStruct((match_count, channels, LANES), jnp.bfloat16)
    outs = (bands, near, own, own, slots)
    return pl.pallas_call(
        functools.partial(prepare_kernel, match_count, taps),
        out_shape=outs,
        in_specs=[VMEM],
        out_specs=(VMEM,) * len(outs),
        scratch_shapes=[pltpu.VMEM((8, 2 * WINDOW), jnp.float32)],
        compiler_params=granted(((WINDOW, 4 * WINDOW), jnp.float32)),
        cost_estimate=pl.CostEstimate(flops=2 * MIB, bytes_accessed=MIB, transcendentals=0),
        name="prepare",
    )(packed)


def normalize_kernel(steps, own_high, own_low, bands_ref, near_ref, *refs):
    blocks, (out_ref, high, low) = refs[:-3], refs[-3:]
    channels, samples_dev = own_high.shape
    count = len(blocks) + 1
    samples = samples_dev * count
    own = lax.axis_index("tm")
    edge = jnp.zeros((channels, LANES), jnp.bfloat16)
    for part in (high, low):
        part[:, :LANES] = edge
        part[:, LANES + samples :] = edge
    for step, block in zip(((0, 0), *steps), (None, *blocks)):
        back = jnp.where(lax.rem(lax.axis_index("chan"), 2) == 0, step[0], step[1])
        place = lax.rem(own + (count - back), count)
        at = pl.ds(pl.multiple_of(LANES + place * samples_dev, LANES), samples_dev)
        if block is None:
            high[:, at], low[:, at] = own_high[...], own_low[...]
        else:
            high[:, at], low[:, at] = split(block[...])
    tiles = samples // LANES

    def windows(part, count):
        return jnp.concatenate(
            [part[:, n * LANES : n * LANES + WINDOW] for n in range(count)], axis=0
        )

    product = mm(windows(high, tiles + 1), bands_ref[...])
    product = product[:, :LANES] + (
        product[:, LANES:] + mm(windows(low, tiles + 1), bands_ref[:, :LANES])
    )
    early = lax.broadcasted_iota(jnp.int32, (channels, LANES), 1) < HALF
    turned = []
    for n in range(tiles + 1):
        filtered = product[n * channels : (n + 1) * channels]
        if n == 0:
            filtered = jnp.where(early, 0.0, filtered)
        if n == tiles:
            filtered = jnp.where(early, filtered, 0.0)
        at = slice(n * LANES, (n + 1) * LANES)
        high[:, at], low[:, at] = split(jnp.abs(filtered))
        turned.append(pltpu.roll(filtered, HALF, 1))
    sums = mm(windows(high, tiles), near_ref[...]) + mm(windows(low, tiles), near_ref[...])
    for n in range(tiles):
        filtered = jnp.where(early, turned[n], turned[n + 1])
        local_mean = sums[n * channels : (n + 1) * channels] * (1.0 / AVG)
        out_ref[:, n * LANES : (n + 1) * LANES] = (filtered / (local_mean + EPSILON)).astype(
            jnp.bfloat16
        )


def normalize(own, banded, steps, blocks):
    channels, samples_dev = own[0].shape
    samples = samples_dev * (len(blocks) + 1)
    padded = (channels, samples + 2 * LANES)
    return pl.pallas_call(
        functools.partial(normalize_kernel, steps),
        out_shape=jax.ShapeDtypeStruct((channels, samples), jnp.bfloat16),
        in_specs=[VMEM] * (len(blocks) + 4),
        out_specs=VMEM,
        scratch_shapes=[pltpu.VMEM(padded, jnp.bfloat16)] * 2,
        compiler_params=granted((padded, jnp.float32), (padded, jnp.float32)),
        name="normalize",
    )(*own, *banded, *blocks)


def lag_kernel(row_share, normed_ref, out_ref):
    first = lax.axis_index("tm") * row_share // ROWS * ROWS
    own = normed_ref[pl.ds(pl.multiple_of(first, ROWS), ROWS), :].astype(jnp.float32)
    own = jnp.concatenate([own, jnp.zeros((ROWS, LANES), jnp.float32)], axis=1)
    last = lax.broadcasted_iota(jnp.int32, (ROWS, LANES), 1) == LANES - 1
    samples = normed_ref.shape[1]
    for turn in range(TURNS + 1):
        moved = pltpu.roll(own, 2 * turn, 1)
        tail = jnp.where(last, moved[:, :LANES], moved[:, samples:])
        at = slice(turn * ROWS, (turn + 1) * ROWS)
        out_ref[at, :samples] = moved[:, :samples].astype(jnp.bfloat16)
        out_ref[at, samples:] = tail.astype(jnp.bfloat16)


def lags_of(normed, row_share):
    shape = ((TURNS + 1) * ROWS, normed.shape[1] + LANES)
    return pl.pallas_call(
        functools.partial(lag_kernel, row_share),
        out_shape=jax.ShapeDtypeStruct(shape, jnp.bfloat16),
        in_specs=[VMEM],
        out_specs=VMEM,
        compiler_params=granted((shape, jnp.bfloat16)),
        cost_estimate=pl.CostEstimate(flops=2 * MIB, bytes_accessed=4 * MIB, transcendentals=0),
        name="lags",
    )(normed)


def correlate_kernel(parcels, picks_ref, lagged, *refs):
    groups, (out_ref, partner, first_end, result, sem) = refs[:parcels], refs[parcels:]
    match_count = picks_ref.shape[0]
    group_ch, samples = groups[0].shape[-2:]
    scaling = 1.0 / math.sqrt(samples)
    pair = 2 * group_ch
    last = lax.broadcasted_iota(jnp.int32, (group_ch, LANES), 1) == LANES - 1

    def take(match, rows):
        even, odd = pl.ds(match * pair, group_ch), pl.ds(match * pair + group_ch, group_ch)
        ahead = pltpu.roll(rows.astype(jnp.float32), samples - 1, 1)
        end = slice(samples - LANES, samples)
        partner[even, :] = rows.astype(jnp.bfloat16)
        partner[odd, : samples - LANES] = ahead[:, : samples - LANES].astype(jnp.bfloat16)
        partner[odd, end] = jnp.where(last, 0.0, ahead[:, end]).astype(jnp.bfloat16)
        first_end[even, :] = jnp.where(last, 0.0, rows[:, end].astype(jnp.float32)).astype(jnp.bfloat16)
        first_end[odd, :] = ahead[:, end].astype(jnp.bfloat16)

    for match in range(match_count):
        if parcels == 1:
            take(match, groups[0][picks_ref[match, lax.axis_index("chan")]])
            continue
        slot = picks_ref[match]
        tiles = []
        for begin in range(0, samples, LANES):
            tile = groups[-1][:, begin : begin + LANES]
            for offset in range(parcels - 1):
                held = groups[offset][:, begin : begin + LANES]
                tile = jnp.where(slot == offset + 1.0, held, tile)
            tiles.append(tile)
        take(match, jnp.concatenate(tiles, axis=1))
    copies = []
    for wrap in (1, 0):
        if wrap == 0:
            partner[:, samples - LANES :] = first_end[...]
        for chunk in range(CHUNKS):
            begin = chunk * TURNS // CHUNKS
            steps = TURNS // CHUNKS + (wrap == 1 and chunk == CHUNKS - 1)
            product = lax.dot_general(
                lagged[begin * ROWS : (begin + steps) * ROWS, pl.ds((1 - wrap) * LANES, samples)],
                partner[...],
                (((1,), (1,)), ((), ())),
                preferred_element_type=jnp.float32,
            )
            product = (product * scaling).astype(jnp.bfloat16)
            left = (wrap * TURNS + begin) * pair
            for step in range(steps):
                column = left + step * pair
                width = min(pair, LAGS * group_ch - column)
                for match in range(match_count):
                    result[match, :, column : column + width] = product[
                        step * ROWS : (step + 1) * ROWS, match * pair : match * pair + width
                    ]
            columns = pl.ds(left, min(steps * pair, LAGS * group_ch - left))
            copy = pltpu.make_async_copy(
                result.at[:, :, columns], out_ref.at[:, :, columns], sem.at[len(copies)]
            )
            copy.start()
            copies.append(copy)
    for copy in copies:
        copy.wait()


def correlate(picks, lagged, groups):
    match_count = picks.shape[0]
    group_ch, samples = groups[0].shape[-2:]
    out = (match_count, ROWS, LAGS * group_ch)
    partner = (2 * match_count * group_ch, samples)
    held = [(g.shape, g.dtype) for g in groups]
    return pl.pallas_call(
        functools.partial(correlate_kernel, len(groups)),
        out_shape=jax.ShapeDtypeStruct(out, jnp.bfloat16),
        in_specs=[SMEM if len(groups) == 1 else VMEM, VMEM] + [VMEM] * len(groups),
        out_specs=pl.BlockSpec(memory_space=pl.ANY),
        scratch_shapes=[
            pltpu.VMEM(partner, jnp.bfloat16),
            pltpu.VMEM((partner[0], LANES), jnp.bfloat16),
            pltpu.VMEM(out, jnp.bfloat16),
            pltpu.SemaphoreType.DMA((2 * CHUNKS,)),
        ],
        compiler_params=granted((lagged.shape, lagged.dtype), (out, jnp.bfloat16), *held),
        name="correlate",
    )(picks, lagged, *groups)


def local(records, fir_taps, matchings):
    group_ch, samples_dev = records.shape
    time_count = lax.axis_size("tm")
    group_count = lax.axis_size("chan")
    row_share = group_ch // time_count

    def turned(cells, step):
        moves = [
            (i * group_count + g, (i + step[g % 2]) % time_count * group_count + g)
            for i in range(time_count)
            for g in range(group_count)
        ]
        return lax.ppermute(cells, ("tm", "chan"), moves)

    def swapped(cells, bit):
        return lax.ppermute(cells, "chan", [(i, i ^ bit) for i in range(group_count)])

    turns = range(1, time_count)
    even = sorted(turns, key=lambda step: (min(step, time_count - step), step % 2 * step))
    odd = sorted(turns, key=lambda step: (-min(step, time_count - step), -step))
    steps = list(zip(even, odd))
    blocks = [turned(records, step) for step in steps]
    *banded, own_high, own_low, slots = prepare(fir_taps, records, matchings)
    normed = normalize((own_high, own_low), banded, steps, blocks)
    if group_count == 4:
        near, far = swapped(normed, 1), swapped(normed, 2)
        picks, groups = slots, [near, far, swapped(far, 1)]
    else:
        picks, groups = matchings, [lax.all_gather(normed, "chan", axis=0)]
    result = correlate(picks, lags_of(normed, row_share), groups)
    if row_share != ROWS:
        begin = lax.axis_index("tm") * row_share
        result = lax.dynamic_slice_in_dim(result, begin % ROWS, row_share, 1)
    return result[:, None]


def solution(mesh):
    in_specs = (P(("parts", "chan"), "tm"), P(), P())
    out_specs = P(None, ("parts", "chan"), "tm", None)
    return jax.shard_map(local, mesh=mesh, in_specs=in_specs, out_specs=out_specs, check_vma=False)
```
